32 devices in a mesh: mp: 2 (over y), dp: 4 (over x, core), seq: 4 (over z).
Axes of the slice: x: 2, y: 2, z: 4, core: 2. Of those that a mesh axis runs over, the one named last changes fastest.
Arguments:
- tokens: bfloat16 [32, 1024, 1024], P('dp', 'seq'), may hold values from -6 to 6
- cotangent: bfloat16 [32, 1024, 1024], P('dp', 'seq'), may hold values from -6 to 6
- lengths: int32 [32], P('dp'), may hold values from 256 to 1024, as said below
- orientation: int32 [32], P('dp'), may hold values from 0 to 1
- joint_weight: float32 [1024, 3072], P(('dp', 'seq'), 'mp'), may hold values from -0.1875 to 0.1875
- output_weight: float32 [1024, 1024], P('mp', ('dp', 'seq')), may hold values from -1 to 1
- expand_weight: float32 [1024, 4096], P(('dp', 'seq'), 'mp'), may hold values from -0.1875 to 0.1875
- shrink_weight: float32 [4096, 1024], P('mp', ('dp', 'seq')), may hold values from -0.09375 to 0.09375
- norm_params: float32 [3, 1024], P(None, 'mp')
- expand_bias: float32 [4096], P('mp'), may hold values from -2 to 2
- norm_moment: float32 [3, 1024], P(None, 'mp'), may hold values from 3276 to 13107
- bias_moment: float32 [4096], P('mp'), may hold values from 204 to 819
- joint_left: float32 [1024, 128], P(('dp', 'seq'), 'mp')
- joint_right: float32 [24576, 3072], P(('dp', 'seq'), 'mp')
- joint_left_root: float32 [1024, 128], P(('dp', 'seq'), 'mp')
- joint_right_root: float32 [24576, 3072], P(('dp', 'seq'), 'mp')
- output_left: float32 [8192, 1024], P(('dp', 'seq'), 'mp')
- output_right: float32 [1024, 128], P(('dp', 'seq'), 'mp')
- output_left_root: float32 [8192, 1024], P(('dp', 'seq'), 'mp')
- output_right_root: float32 [1024, 128], P(('dp', 'seq'), 'mp')
- expand_left: float32 [1024, 128], P(('dp', 'seq'), 'mp')
- expand_right: float32 [32768, 4096], P(('dp', 'seq'), 'mp')
- expand_left_root: float32 [1024, 128], P(('dp', 'seq'), 'mp')
- expand_right_root: float32 [32768, 4096], P(('dp', 'seq'), 'mp')
- shrink_left: float32 [32768, 4096], P(('dp', 'seq'), 'mp')
- shrink_right: float32 [1024, 128], P(('dp', 'seq'), 'mp')
- shrink_left_root: float32 [32768, 4096], P(('dp', 'seq'), 'mp')
- shrink_right_root: float32 [1024, 128], P(('dp', 'seq'), 'mp')
Outputs:
- block_output: bfloat16 [32, 1024, 1024], P('dp', 'seq', 'mp')
- input_grad: float32 [32, 1024, 1024], P('dp', 'seq')
- joint_grad: float32 [1024, 3072], P(('dp', 'seq'), 'mp')
- output_grad: float32 [1024, 1024], P('mp', ('dp', 'seq'))
- expand_grad: float32 [1024, 4096], P(('dp', 'seq'), 'mp')
- shrink_grad: float32 [4096, 1024], P('mp', ('dp', 'seq'))
- norm_grad: float32 [3, 1024], P(None, 'mp')
- bias_grad: float32 [4096], P('mp')
- joint_left_new: float32 [1024, 128], P(('dp', 'seq'), 'mp')
- joint_right_new: float32 [24576, 3072], P(('dp', 'seq'), 'mp')
- output_left_new: float32 [8192, 1024], P(('dp', 'seq'), 'mp')
- output_right_new: float32 [1024, 128], P(('dp', 'seq'), 'mp')
- expand_left_new: float32 [1024, 128], P(('dp', 'seq'), 'mp')
- expand_right_new: float32 [32768, 4096], P(('dp', 'seq'), 'mp')
- shrink_left_new: float32 [32768, 4096], P(('dp', 'seq'), 'mp')
- shrink_right_new: float32 [1024, 128], P(('dp', 'seq'), 'mp')
- joint_weight_new: float32 [1024, 3072], P(('dp', 'seq'), 'mp')
- output_weight_new: float32 [1024, 1024], P('mp', ('dp', 'seq'))
- expand_weight_new: float32 [1024, 4096], P(('dp', 'seq'), 'mp')
- shrink_weight_new: float32 [4096, 1024], P('mp', ('dp', 'seq'))
- norm_moment_new: float32 [3, 1024], P(None, 'mp')
- bias_moment_new: float32 [4096], P('mp')
- norm_params_new: float32 [3, 1024], P(None, 'mp')
- bias_new: float32 [4096], P('mp')
The draws below stay inside these ranges and needn't reach their ends.
Inputs may be any that keep to these rules, and one draw needn't show every extreme that they name: `lengths`: sequences 0 to 7, 8 to 15 and so on each hold at least one of length 1024. `orientation`: 1 marks a reversed protein, whose padding stands before position 1024 - lengths; 0 a forward one, padded after lengths - 1.
All inputs are finite; a program needn't handle non-finite values.
Results may differ from the reference program's by a relative error of at most 0.005.
The reference program's roundings to bfloat16 on the way count: a program that leaves them out, or rounds other values in their place, can miss the bound.
Values may be sent and summed in bfloat16 or wider, within the bound.
No kernel may reach another device: no remote copies, remote signals or barrier semaphores. Data moves between devices by JAX's collectives and lax.ppermute only.
A program may use at most 512 MiB of HBM per device.

```python
import math
import jax
import jax.numpy as jnp
from jax import lax

D = 1024
HEADS = 16
HS = 64
ROT = 32
FF = 4096
LEN = 1024
SEQS_DP = 8
SEQS = 32
OWNERS = 16
RB = 64
CQ = 1536
CA = 512
CF = 2048
TOKENS_ALL = 32768
N_MP = 2
N_DP = 4


def square_blocks(key, size, scale):
    key_diag, key_off = jax.random.split(key)
    diagonal = scale * jnp.exp(jax.random.uniform(key_diag, (OWNERS, N_MP, size), jnp.float32, 0.0, math.log(4.0)))
    rough = jax.random.uniform(key_off, (OWNERS, N_MP, size, size), jnp.float32, -1.0, 1.0)
    symmetric = (rough + jnp.swapaxes(rough, -1, -2)) * (0.6 * scale / math.sqrt(size))
    identity = jnp.eye(size, dtype=jnp.float32)
    blocks = symmetric * (1.0 - identity) + diagonal[..., :, None] * identity
    return jnp.transpose(blocks, (0, 2, 1, 3)).reshape(OWNERS * size, N_MP * size)


def draw_lengths(key, part):
    key = jax.random.fold_in(key, 1)
    key_len, key_pick = jax.random.split(key)
    drawn = jax.random.randint(key_len, (N_DP, SEQS_DP), LEN // 4, LEN + 1)
    picked = jax.random.randint(key_pick, (N_DP, 1), 0, SEQS_DP)
    full_one = jnp.arange(SEQS_DP)[None, :] == picked
    return jnp.where(full_one, LEN, drawn).reshape(SEQS).astype(jnp.int32)


def draw_norm_params(key, part):
    key = jax.random.fold_in(key, 2)
    key_gain, key_rest = jax.random.split(key)
    gain_row = 1.0 + jax.random.uniform(key_gain, (1, D), jnp.float32, -0.3, 0.3)
    rest_rows = 0.3 * jnp.clip(jax.random.normal(key_rest, (2, D), jnp.float32), -4.0, 4.0)
    return jnp.concatenate([gain_row, rest_rows], axis=0)


def draw_joint_left(key, part):
    return square_blocks(jax.random.fold_in(key, 11), RB, CQ * TOKENS_ALL / 38.0)


def draw_joint_right(key, part):
    return square_blocks(jax.random.fold_in(key, 12), CQ, RB * TOKENS_ALL / 38.0)


def draw_joint_left_root(key, part):
    return square_blocks(jax.random.fold_in(key, 13), RB, (CQ * TOKENS_ALL / 38.0) ** (-0.25))


def draw_joint_right_root(key, part):
    return square_blocks(jax.random.fold_in(key, 14), CQ, (RB * TOKENS_ALL / 38.0) ** (-0.25))


def draw_output_left(key, part):
    return square_blocks(jax.random.fold_in(key, 21), CA, RB * TOKENS_ALL / 950.0)


def draw_output_right(key, part):
    return square_blocks(jax.random.fold_in(key, 22), RB, CA * TOKENS_ALL / 950.0)


def draw_output_left_root(key, part):
    return square_blocks(jax.random.fold_in(key, 23), CA, (RB * TOKENS_ALL / 950.0) ** (-0.25))


def draw_output_right_root(key, part):
    return square_blocks(jax.random.fold_in(key, 24), RB, (CA * TOKENS_ALL / 950.0) ** (-0.25))


def draw_expand_left(key, part):
    return square_blocks(jax.random.fold_in(key, 31), RB, CF * TOKENS_ALL / 152.0)


def draw_expand_right(key, part):
    return square_blocks(jax.random.fold_in(key, 32), CF, RB * TOKENS_ALL / 152.0)


def draw_expand_left_root(key, part):
    return square_blocks(jax.random.fold_in(key, 33), RB, (CF * TOKENS_ALL / 152.0) ** (-0.25))


def draw_expand_right_root(key, part):
    return square_blocks(jax.random.fold_in(key, 34), CF, (RB * TOKENS_ALL / 152.0) ** (-0.25))


def draw_shrink_left(key, part):
    return square_blocks(jax.random.fold_in(key, 41), CF, RB * TOKENS_ALL / 45.0)


def draw_shrink_right(key, part):
    return square_blocks(jax.random.fold_in(key, 42), RB, CF * TOKENS_ALL / 45.0)


def draw_shrink_left_root(key, part):
    return square_blocks(jax.random.fold_in(key, 43), CF, (RB * TOKENS_ALL / 45.0) ** (-0.25))


def draw_shrink_right_root(key, part):
    return square_blocks(jax.random.fold_in(key, 44), RB, (CF * TOKENS_ALL / 45.0) ** (-0.25))


def place_ends(array, key, low, top_value):
    spot = [jax.random.randint(jax.random.fold_in(key, axis), (), 0, length) for axis, length in enumerate(array.shape)]
    widest = array.shape.index(max(array.shape))
    next_to = spot[:widest] + [(spot[widest] + 1) % array.shape[widest]] + spot[widest + 1:]
    return array.at[tuple(spot)].set(low).at[tuple(next_to)].set(top_value)


def levels(rng, dims, cuts, smallest, top_value):
    def one(dim, shards_of):
        draws = jax.random.uniform(jax.random.fold_in(jax.random.fold_in(rng, 6), dim), (shards_of,), jnp.float32, smallest / len(cuts), top_value / len(cuts))
        return jnp.repeat(jnp.exp(draws), dims[dim] // shards_of).reshape((-1,) + (1,) * (len(dims) - dim - 1))

    level = one(*cuts[0])
    for cut in cuts[1:]:
        level = level * one(*cut)
    return level


def scatter_about(rng, extent, scale, most, shards=(), kind=jnp.bfloat16):
    values = scale * jax.random.normal(rng, extent, jnp.float32)
    if shards:
        values = values * levels(rng, extent, shards, -0.22, 0.18)
    return jnp.clip(values, -most, most).astype(kind)


def setup_inputs(seed: int = 0) -> dict:
    key_list = jax.random.split(jax.random.key(seed), 29)
    tokens = scatter_about(key_list[0], (SEQS, LEN, D), 1.0, 6.0, ((0, 4), (1, 4)))
    cotangent = scatter_about(key_list[1], (SEQS, LEN, D), 1.0, 6.0, ((0, 4), (1, 4)))
    lengths = draw_lengths(jax.random.fold_in(key_list[28], 71), 0)
    orientation = place_ends(jax.random.randint(key_list[3], (SEQS,), 0, 2), jax.random.fold_in(key_list[3], 1), 0, 1).astype(jnp.int32)
    joint_weight = scatter_about(key_list[4], (D, 3 * HEADS * HS), D ** -0.5, 0.1875, ((0, 16), (1, 2)), jnp.float32)
    output_weight = scatter_about(key_list[5], (HEADS * HS, D), (D // 32) ** -0.5, 1.0, ((0, 2), (1, 16)), jnp.float32)
    expand_weight = scatter_about(key_list[6], (D, FF), D ** -0.5, 0.1875, ((0, 16), (1, 2)), jnp.float32)
    shrink_weight = scatter_about(key_list[7], (FF, D), FF ** -0.5, 0.09375, ((0, 2), (1, 16)), jnp.float32)
    norm_params = draw_norm_params(jax.random.fold_in(key_list[28], 71), 0)
    expand_bias = scatter_about(key_list[9], (FF,), 0.3, 2.0, ((0, 2),), jnp.float32)
    norm_moment = jnp.clip(jnp.exp(math.log(13107.0) - 1.3865233 * jax.random.uniform(key_list[10], (3, D), jnp.float32) ** levels(key_list[10], (3, D), ((1, 2),), -0.2, 0.2)), 3276.0, 13107.0)
    bias_moment = jnp.clip(jnp.exp(math.log(819.0) - 1.3899641 * jax.random.uniform(key_list[11], (FF,), jnp.float32) ** levels(key_list[11], (FF,), ((0, 2),), -0.2, 0.2)), 204.0, 819.0)
    joint_left = draw_joint_left(jax.random.fold_in(key_list[28], 71), 0)
    joint_right = draw_joint_right(jax.random.fold_in(key_list[28], 71), 0)
    joint_left_root = draw_joint_left_root(jax.random.fold_in(key_list[28], 71), 0)
    joint_right_root = draw_joint_right_root(jax.random.fold_in(key_list[28], 71), 0)
    output_left = draw_output_left(jax.random.fold_in(key_list[28], 71), 0)
    output_right = draw_output_right(jax.random.fold_in(key_list[28], 71), 0)
    output_left_root = draw_output_left_root(jax.random.fold_in(key_list[28], 71), 0)
    output_right_root = draw_output_right_root(jax.random.fold_in(key_list[28], 71), 0)
    expand_left = draw_expand_left(jax.random.fold_in(key_list[28], 71), 0)
    expand_right = draw_expand_right(jax.random.fold_in(key_list[28], 71), 0)
    expand_left_root = draw_expand_left_root(jax.random.fold_in(key_list[28], 71), 0)
    expand_right_root = draw_expand_right_root(jax.random.fold_in(key_list[28], 71), 0)
    shrink_left = draw_shrink_left(jax.random.fold_in(key_list[28], 71), 0)
    shrink_right = draw_shrink_right(jax.random.fold_in(key_list[28], 71), 0)
    shrink_left_root = draw_shrink_left_root(jax.random.fold_in(key_list[28], 71), 0)
    shrink_right_root = draw_shrink_right_root(jax.random.fold_in(key_list[28], 71), 0)
    return {"tokens": tokens, "cotangent": cotangent, "lengths": lengths, "orientation": orientation, "joint_weight": joint_weight, "output_weight": output_weight, "expand_weight": expand_weight, "shrink_weight": shrink_weight, "norm_params": norm_params, "expand_bias": expand_bias, "norm_moment": norm_moment, "bias_moment": bias_moment, "joint_left": joint_left, "joint_right": joint_right, "joint_left_root": joint_left_root, "joint_right_root": joint_right_root, "output_left": output_left, "output_right": output_right, "output_left_root": output_left_root, "output_right_root": output_right_root, "expand_left": expand_left, "expand_right": expand_right, "expand_left_root": expand_left_root, "expand_right_root": expand_right_root, "shrink_left": shrink_left, "shrink_right": shrink_right, "shrink_left_root": shrink_left_root, "shrink_right_root": shrink_right_root}


@jax.custom_vjp
def low(v):
    return lax.optimization_barrier(v.astype(jnp.bfloat16)).astype(jnp.float32)

@jax.custom_vjp
def low_back(v):
    return v

def low_keep(v):
    return (low(v), None)

def low_pass(kept, grad):
    return (grad,)

def back_keep(v):
    return (v, None)

def back_low(kept, grad):
    return (low(grad),)
low.defvjp(low_keep, low_pass)
low_back.defvjp(back_keep, back_low)
highest = lax.Precision.HIGHEST
norm_eps = 1e-05
beta_stats = 0.95
beta_moment = 0.95
rate_matrix = 0.5
rate_vector = 0.03

def rotate(values, positions):
    half_rot = ROT // 2
    frequency = 10000.0 ** (-2.0 * jnp.arange(half_rot, dtype=jnp.float32) / ROT)
    angles = positions[:, None] * frequency[None, :]
    cosine = jnp.cos(angles)[:, None, :]
    sine_part = jnp.sin(angles)[:, None, :]
    paired = values[..., :ROT].reshape(values.shape[:-1] + (half_rot, 2))
    even_part = paired[..., 0]
    odd_part = paired[..., 1]
    turned = jnp.stack([even_part * cosine - odd_part * sine_part, odd_part * cosine + even_part * sine_part], axis=-1)
    return jnp.concatenate([turned.reshape(values.shape[:-1] + (ROT,)), values[..., ROT:]], axis=-1)

def allowed_keys(positions, length, reversed_one):
    valid = jnp.where(reversed_one == 0, positions < length, positions >= LEN - length)
    causal = positions[None, :] <= positions[:, None]
    itself = positions[None, :] == positions[:, None]
    return causal & (valid[None, :] | itself)

def layer(params, inputs, lengths, orientation):
    joint_w, output_w, expand_w, shrink_w, vectors, bias_in = params
    group_size = inputs.shape[0]
    centred = inputs - lax.optimization_barrier(jnp.mean(inputs, -1, keepdims=True))
    spread = lax.optimization_barrier(jnp.mean(centred * centred, -1, keepdims=True))
    normed = low(centred * lax.rsqrt(spread + norm_eps) * vectors[0] + vectors[1])
    joint_cols = low_back(jnp.einsum('gtd,dc->gtc', normed, joint_w, precision=highest))
    heads_dev = HEADS // N_MP
    joint_cols = joint_cols.reshape(group_size, LEN, N_MP, 3, heads_dev, HS)
    positions = jnp.arange(LEN).astype(jnp.float32)
    queries = low(rotate(joint_cols[:, :, :, 0].reshape(group_size, LEN, HEADS, HS), positions))
    keys_all = low(rotate(joint_cols[:, :, :, 1].reshape(group_size, LEN, HEADS, HS), positions))
    values_all = low(joint_cols[:, :, :, 2].reshape(group_size, LEN, HEADS, HS))
    position_ids = jnp.arange(LEN, dtype=jnp.int32)
    score_scale = 1.0 / math.sqrt(HS)

    def attend(sequence):
        query_one, key_one, value_one, length, reversed_one = sequence
        scores = low_back(jnp.einsum('qhd,khd->hqk', query_one, key_one, precision=highest) * score_scale)
        allowed = allowed_keys(position_ids, length, reversed_one)[None]
        masked = jnp.where(allowed, scores, -1e+30)
        row_top = lax.optimization_barrier(jnp.max(masked, -1, keepdims=True))
        exponent = jnp.where(allowed, jnp.exp(masked - row_top), 0.0)
        weights = low(exponent / lax.optimization_barrier(jnp.sum(exponent, -1, keepdims=True)))
        return jnp.einsum('hqk,khd->qhd', weights, value_one, precision=highest)
    context = lax.map(jax.checkpoint(attend), (queries, keys_all, values_all, lengths, orientation))
    context = low(low_back(context.reshape(group_size, LEN, HEADS * HS)))
    pre_act = low_back(jnp.einsum('gtd,df->gtf', normed, expand_w, precision=highest) + bias_in)
    active = low(jax.nn.gelu(pre_act, approximate=True))
    branch = jnp.einsum('gtc,cd->gtd', context, output_w, precision=highest)
    branch = branch + jnp.einsum('gtf,fd->gtd', active, shrink_w, precision=highest)
    return inputs + branch + vectors[2]

def shampoo(grad4, weight4, left, right, left_root, right_root, fan):
    a_size = grad4.shape[1]
    b_size = grad4.shape[3]
    left4 = left.reshape(OWNERS, a_size, N_MP, a_size)
    right4 = right.reshape(OWNERS, b_size, N_MP, b_size)
    left_root4 = left_root.reshape(OWNERS, a_size, N_MP, a_size)
    right_root4 = right_root.reshape(OWNERS, b_size, N_MP, b_size)
    left_new = beta_stats * left4 + (1.0 - beta_stats) * jnp.einsum('iajb,icjb->iajc', grad4, grad4, precision=highest)
    right_new = beta_stats * right4 + (1.0 - beta_stats) * jnp.einsum('iajb,iajc->ibjc', grad4, grad4, precision=highest)
    first_side = jnp.einsum('iajc,icjb->iajb', left_root4, grad4, precision=highest)
    turned = jnp.einsum('iajc,icjb->iajb', first_side, right_root4, precision=highest)
    square = lax.optimization_barrier(jnp.mean(turned * turned, axis=(1, 3), keepdims=True))
    weight_new = weight4 - rate_matrix / math.sqrt(fan) * turned * lax.rsqrt(square + 1e-06)
    return (left_new.reshape(left.shape), right_new.reshape(right.shape), weight_new)

def row_blocks(matrix, cols):
    return matrix.reshape(OWNERS, RB, N_MP, cols)

def col_blocks(matrix, rows_each):
    return jnp.transpose(matrix.reshape(N_MP, rows_each, OWNERS, RB), (2, 1, 0, 3))

def diagonal_rule(params, moment, gradient):
    moment_new = beta_moment * moment + (1.0 - beta_moment) * gradient * gradient
    return (moment_new, params - rate_vector * gradient / (jnp.sqrt(moment_new) + 1e-08))

def reference(tokens, cotangent, lengths, orientation, joint_weight, output_weight, expand_weight, shrink_weight, norm_params, expand_bias, norm_moment, bias_moment, joint_left, joint_right, joint_left_root, joint_right_root, output_left, output_right, output_left_root, output_right_root, expand_left, expand_right, expand_left_root, expand_right_root, shrink_left, shrink_right, shrink_left_root, shrink_right_root):
    params = (joint_weight.astype(jnp.bfloat16).astype(jnp.float32), output_weight.astype(jnp.bfloat16).astype(jnp.float32), expand_weight.astype(jnp.bfloat16).astype(jnp.float32), shrink_weight.astype(jnp.bfloat16).astype(jnp.float32), norm_params, expand_bias)
    groups = SEQS // 4
    token_groups = tokens.reshape(groups, 4, LEN, D)
    cot_groups = cotangent.reshape(groups, 4, LEN, D)
    length_groups = lengths.reshape(groups, 4)
    orient_groups = orientation.reshape(groups, 4)
    zeros = jax.tree.map(jnp.zeros_like, params)

    def scan_step(totals, inputs_one):
        token_one, cot_one, length_one, orient_one = inputs_one

        def forward(param_set, values):
            return layer(param_set, values, length_one, orient_one)
        output_one, pull_back = jax.vjp(forward, params, token_one.astype(jnp.float32))
        param_grads, input_grad_one = pull_back(cot_one.astype(jnp.float32))
        totals = jax.tree.map(jnp.add, totals, param_grads)
        return (totals, (output_one.astype(jnp.bfloat16), input_grad_one))
    gradients, (outputs, input_grads) = lax.scan(scan_step, zeros, (token_groups, cot_groups, length_groups, orient_groups))
    joint_grad, output_grad, expand_grad, shrink_grad, norm_grad, bias_grad = gradients
    block_output = outputs.reshape(SEQS, LEN, D)
    input_grad = input_grads.reshape(SEQS, LEN, D)
    joint_left_new, joint_right_new, joint_new4 = shampoo(row_blocks(joint_grad, CQ), row_blocks(joint_weight, CQ), joint_left, joint_right, joint_left_root, joint_right_root, D)
    expand_left_new, expand_right_new, expand_new4 = shampoo(row_blocks(expand_grad, CF), row_blocks(expand_weight, CF), expand_left, expand_right, expand_left_root, expand_right_root, D)
    output_left_new, output_right_new, output_new4 = shampoo(col_blocks(output_grad, CA), col_blocks(output_weight, CA), output_left, output_right, output_left_root, output_right_root, D // 32)
    shrink_left_new, shrink_right_new, shrink_new4 = shampoo(col_blocks(shrink_grad, CF), col_blocks(shrink_weight, CF), shrink_left, shrink_right, shrink_left_root, shrink_right_root, FF)
    joint_weight_new = joint_new4.reshape(D, 3 * HEADS * HS)
    expand_weight_new = expand_new4.reshape(D, FF)
    output_weight_new = jnp.transpose(output_new4, (2, 1, 0, 3)).reshape(HEADS * HS, D)
    shrink_weight_new = jnp.transpose(shrink_new4, (2, 1, 0, 3)).reshape(FF, D)
    norm_moment_new, norm_params_new = diagonal_rule(norm_params, norm_moment, norm_grad)
    bias_moment_new, bias_new = diagonal_rule(expand_bias, bias_moment, bias_grad)
    return (block_output, input_grad, joint_grad, output_grad, expand_grad, shrink_grad, norm_grad, bias_grad, joint_left_new, joint_right_new, output_left_new, output_right_new, expand_left_new, expand_right_new, shrink_left_new, shrink_right_new, joint_weight_new, output_weight_new, expand_weight_new, shrink_weight_new, norm_moment_new, bias_moment_new, norm_params_new, bias_new)
```

```python
import functools
import math

import jax
import jax.numpy as jnp
from jax import lax
from jax.experimental import pallas as pl
from jax.experimental.pallas import tpu as pltpu
from jax.sharding import PartitionSpec as P

HS = 64
ROT = 32
LEN = 1024
BLOCK = 256

highest = lax.Precision.HIGHEST
norm_eps = 1e-05
beta_stats = 0.95
beta_moment = 0.95
rate_matrix = 0.5
rate_vector = 0.03
bf16 = jnp.bfloat16
f32 = jnp.float32
NT = (((1,), (1,)), ((), ()))
TN = (((0,), (0,)), ((), ()))
NN = (((1,), (0,)), ((), ()))


def mm(a, b, dims=NN):
    return lax.dot_general(a, b, dims, preferred_element_type=f32)


def bits_of(size):
    return [1 << i for i in range(size.bit_length() - 1)]


def swap(value, axis, bit):
    size = lax.axis_size(axis)
    return lax.ppermute(value, axis, [(i, i ^ bit) for i in range(size)])


def gather_rows(shard):
    rows, cols = shard.shape
    value = shard[None]
    for axis in ("seq", "dp"):
        inner = value.shape
        lead = 1
        for bit in reversed(bits_of(lax.axis_size(axis))):
            other = swap(value, axis, bit)
            upper = (lax.axis_index(axis) & bit) != 0
            value = jnp.stack([jnp.where(upper, other, value), jnp.where(upper, value, other)], axis=1)
            value = value.reshape((lead * 2,) + inner)
            lead *= 2
        value = value.reshape((1, -1, cols))
    return value.reshape(-1, cols)


def scatter_rows(term, kind=bf16):
    cols = term.shape[1]
    n_dp, n_seq = lax.axis_size("dp"), lax.axis_size("seq")
    value = term.reshape(1, n_dp, -1)
    for axis, size in (("dp", n_dp), ("seq", n_seq)):
        value = value.reshape(size, -1, cols)
        for bit in bits_of(size):
            parts = value.reshape((value.shape[0] // 2, 2) + value.shape[1:])
            index = (lax.axis_index(axis) & bit) // bit
            mine = lax.dynamic_index_in_dim(parts, index, 1, False)
            theirs = lax.dynamic_index_in_dim(parts, 1 - index, 1, False)
            value = mine + swap(theirs.astype(kind), axis, bit).astype(f32)
    return value.reshape(-1, cols)


def sum_all(value, axes):
    for axis in axes:
        for bit in bits_of(lax.axis_size(axis)):
            value = value + swap(value, axis, bit)
    return value


def params(limit=100, **more):
    return pltpu.CompilerParams(vmem_limit_bytes=limit * 2**20 // 2, **more)


def rope_tables():
    lane = jnp.arange(128, dtype=jnp.int32) % HS
    pair = (lane // 2).astype(f32)
    frequency = 10000.0 ** (-2.0 * pair / ROT)
    angles = jnp.arange(LEN, dtype=f32)[:, None] * frequency[None, :]
    turned = (lane < ROT)[None, :]
    cosine = jnp.where(turned, jnp.cos(angles), 1.0)
    sine = jnp.sin(angles)
    to_even = jnp.where(turned & (lane % 2 == 0)[None, :], -sine, 0.0)
    to_odd = jnp.where(turned & (lane % 2 == 1)[None, :], sine, 0.0)
    return cosine, to_even, to_odd


def turn(value, cosine, to_even, to_odd):
    return (
        value * cosine
        + pltpu.roll(value, 127, 1) * to_even
        + pltpu.roll(value, 1, 1) * to_odd
    )


def project_kernel(x_ref, w_ref, c_ref, e_ref, o_ref, out_ref):
    cols = w_ref.shape[1]
    part = cols // 3
    values = mm(x_ref[...], w_ref[...])
    cosine, to_even, to_odd = c_ref[...], e_ref[...], o_ref[...]
    for at in range(0, cols, 128):
        piece = values[:, at : at + 128]
        if at < 2 * part:
            piece = turn(piece, cosine, to_even, to_odd)
        out_ref[:, at : at + 128] = piece.astype(bf16)


def project(rows, weight, tables):
    count, width = rows.shape
    cols = weight.shape[1]
    table = pl.BlockSpec((BLOCK, 128), lambda i: (i, 0))
    return pl.pallas_call(
        project_kernel,
        grid=(count // BLOCK,),
        in_specs=[
            pl.BlockSpec((BLOCK, width), lambda i: (i, 0)),
            pl.BlockSpec((width, cols), lambda i: (0, 0)),
            table,
            table,
            table,
        ],
        out_specs=pl.BlockSpec((BLOCK, cols), lambda i: (i, 0)),
        out_shape=jax.ShapeDtypeStruct((count, cols), bf16),
        compiler_params=params(),
        cost_estimate=pl.CostEstimate(
            flops=2 * count * width * cols, bytes_accessed=2 * (count * (width + cols) + width * cols), transcendentals=0
        ),
        name="project",
    )(rows, weight, *tables)


def attend_kernel(seq_ref, q_ref, k_ref, v_ref, d_ref, c_ref, e_ref, o_ref, ctx_ref, grad_ref, dk_ref, dv_ref):
    part = grad_ref.shape[1] // 3
    pair = pl.program_id(0)
    length, reverse = seq_ref[0], seq_ref[1]
    lane = lax.broadcasted_iota(jnp.int32, (1, 128), 1)
    zero = jnp.zeros((), bf16)
    keys, values = k_ref[...], v_ref[...]
    key_heads, value_heads = [], []
    for head in range(2):
        inside = (lane // HS) == head
        key_heads.append(jnp.where(inside, keys, zero))
        value_heads.append(jnp.where(inside, values, zero))
    dk_ref[...] = jnp.zeros_like(dk_ref)
    dv_ref[...] = jnp.zeros_like(dv_ref)

    low = jnp.where(reverse == 0, 0, LEN - length)
    high = jnp.where(reverse == 0, length, LEN)

    def key_bias(start, size):
        spot = start + lax.broadcasted_iota(jnp.int32, (1, size), 1)
        return jnp.where((spot >= low) & (spot < high), 0.0, -1e30)

    for block in range(LEN // BLOCK):
        begin = block * BLOCK
        stop = begin + BLOCK
        rows = pl.ds(begin, BLOCK)
        query = q_ref[rows, :] * jnp.asarray(1.0 / math.sqrt(HS), bf16)
        back = d_ref[rows, :]
        below = key_bias(0, begin) if begin else None
        q_id = lax.broadcasted_iota(jnp.int32, (BLOCK, BLOCK), 0)
        k_id = lax.broadcasted_iota(jnp.int32, (BLOCK, BLOCK), 1)
        at_diag = jnp.where(k_id < q_id, key_bias(begin, BLOCK), jnp.where(k_id == q_id, 0.0, -1e30))
        context = jnp.zeros((BLOCK, 128), f32)
        grad_query = jnp.zeros((BLOCK, 128), f32)
        for head in range(2):
            inside = (lane // HS) == head
            query_one = jnp.where(inside, query, zero)
            back_one = jnp.where(inside, back, zero)
            scores = mm(query_one, keys[:stop], NT)
            tail = scores[:, begin:] + at_diag
            scores = jnp.concatenate([scores[:, :begin] + below, tail], axis=1) if begin else tail
            top = jnp.max(scores, axis=1, keepdims=True)
            exponent = jnp.exp(scores - top)
            attend = exponent * (1.0 / jnp.sum(exponent, axis=1, keepdims=True))
            attend_low = attend.astype(bf16)
            context += mm(attend_low, value_heads[head][:stop])
            back_attend = mm(back_one, values[:stop], NT)
            delta = jnp.sum(attend * back_attend, axis=1, keepdims=True)
            grad_scores = (attend * (back_attend - delta)).astype(bf16)
            grad_query += mm(grad_scores, key_heads[head][:stop])
            dk_ref[:stop, :] += mm(grad_scores, query_one, TN)
            dv_ref[:stop, :] += mm(attend_low, back_one, TN)
        ctx_ref[rows, :] = context.astype(bf16)
        grad_query = grad_query * (1.0 / math.sqrt(HS))
        grad_query = turn(grad_query, c_ref[rows, :], -e_ref[rows, :], -o_ref[rows, :])
        grad_ref[rows, pl.ds(pl.multiple_of(pair * 128, 128), 128)] = grad_query.astype(bf16)
    grad_key = turn(dk_ref[...], c_ref[...], -e_ref[...], -o_ref[...])
    grad_ref[:, pl.ds(pl.multiple_of(part + pair * 128, 128), 128)] = grad_key.astype(bf16)
    grad_ref[:, pl.ds(pl.multiple_of(2 * part + pair * 128, 128), 128)] = dv_ref[...].astype(bf16)


def attend(info, joint_rows, back_rows, tables):
    cols = joint_rows.shape[1]
    part = cols // 3
    pairs = part // 128
    column = lambda group: pl.BlockSpec((LEN, 128), lambda i, s: (0, group * pairs + i))
    table = pl.BlockSpec((LEN, 128), lambda i, s: (0, 0))
    area = LEN * (LEN + BLOCK) // 2 * (part // HS)
    return pl.pallas_call(
        attend_kernel,
        grid_spec=pltpu.PrefetchScalarGridSpec(
            num_scalar_prefetch=1,
            grid=(pairs,),
            in_specs=[column(0), column(1), column(2), column(0), table, table, table],
            out_specs=[
                pl.BlockSpec((LEN, 128), lambda i, s: (0, i)),
                pl.BlockSpec((LEN, cols), lambda i, s: (0, 0)),
            ],
            scratch_shapes=[pltpu.VMEM((LEN, 128), f32), pltpu.VMEM((LEN, 128), f32)],
        ),
        out_shape=[
            jax.ShapeDtypeStruct((LEN, part), bf16),
            jax.ShapeDtypeStruct((LEN, cols), bf16),
        ],
        compiler_params=params(),
        cost_estimate=pl.CostEstimate(flops=12 * area * 256, bytes_accessed=16 * LEN * part, transcendentals=area),
        name="attend",
    )(info, joint_rows, joint_rows, joint_rows, back_rows, *tables)


def norm_kernel(flip_ref, x_ref, vec_ref, out_ref, own_ref):
    values = x_ref[0].astype(f32)
    centred = values - jnp.mean(values, -1, keepdims=True)
    spread = jnp.mean(centred * centred, -1, keepdims=True)
    normed = centred * lax.rsqrt(spread + norm_eps) * vec_ref[0:1, :] + vec_ref[1:2, :]
    low = normed.astype(bf16)
    out_ref[0] = low

    @pl.when(lax.rem(pl.program_id(0), 2) == flip_ref[0])
    def _():
        own_ref[0] = low


def norm(tokens, vectors, flip):
    seqs, local, width = tokens.shape
    return pl.pallas_call(
        norm_kernel,
        grid_spec=pltpu.PrefetchScalarGridSpec(
            num_scalar_prefetch=1,
            grid=(seqs,),
            in_specs=[
                pl.BlockSpec((1, local, width), lambda i, s: (i, 0, 0)),
                pl.BlockSpec(vectors.shape, lambda i, s: (0, 0)),
            ],
            out_specs=[
                pl.BlockSpec((1, local, width), lambda i, s: (i, 0, 0)),
                pl.BlockSpec((1, local, width), lambda i, s: (i // 2, 0, 0)),
            ],
        ),
        out_shape=[
            jax.ShapeDtypeStruct(tokens.shape, bf16),
            jax.ShapeDtypeStruct((seqs // 2, local, width), bf16),
        ],
        compiler_params=params(),
        cost_estimate=pl.CostEstimate(flops=8 * tokens.size, bytes_accessed=5 * tokens.size, transcendentals=0),
        name="norm",
    )(flip, tokens, vectors)


def norm_back_kernel(order_ref, x_ref, cot_ref, back_ref, vec_ref, *rest):
    out_ref, sums_ref = rest[-2:]
    values = x_ref[0].astype(f32)
    centred = values - jnp.mean(values, -1, keepdims=True)
    spread = jnp.mean(centred * centred, -1, keepdims=True)
    scale = lax.rsqrt(spread + norm_eps)
    xhat = centred * scale
    back = back_ref[0].astype(f32)
    scaled = back * vec_ref[0:1, :]
    shift = jnp.mean(scaled, -1, keepdims=True)
    slope = jnp.mean(scaled * xhat, -1, keepdims=True)
    cot = cot_ref[0].astype(f32)
    out_ref[0] = cot + (scaled - shift - xhat * slope) * scale

    @pl.when(pl.program_id(0) == 0)
    def _():
        sums_ref[...] = jnp.zeros_like(sums_ref)

    sums_ref[0:1, :] += jnp.sum(back * xhat, 0, keepdims=True)
    sums_ref[1:2, :] += jnp.sum(back, 0, keepdims=True)
    sums_ref[2:3, :] += jnp.sum(cot, 0, keepdims=True)


def norm_back(order, tokens, cotangent, back_normed, vectors, earlier=None):
    seqs, local, width = tokens.shape
    count = back_normed.shape[0]
    picked = pl.BlockSpec((1, local, width), lambda i, s: (s[i], 0, 0))
    more = [] if earlier is None else [earlier]
    return pl.pallas_call(
        norm_back_kernel,
        grid_spec=pltpu.PrefetchScalarGridSpec(
            num_scalar_prefetch=1,
            grid=(count,),
            in_specs=[
                picked,
                picked,
                pl.BlockSpec((1, local, width), lambda i, s: (i, 0, 0)),
                pl.BlockSpec(vectors.shape, lambda i, s: (0, 0)),
            ]
            + [pl.BlockSpec(memory_space=pl.ANY)] * len(more),
            out_specs=[picked, pl.BlockSpec((8, width), lambda i, s: (0, 0))],
        ),
        out_shape=[
            jax.ShapeDtypeStruct(tokens.shape, f32),
            jax.ShapeDtypeStruct((8, width), f32),
        ],
        input_output_aliases={5: 0} if more else {},
        compiler_params=params(),
        cost_estimate=pl.CostEstimate(
            flops=30 * back_normed.size, bytes_accessed=10 * back_normed.size, transcendentals=0
        ),
        name="norm_back",
    )(order, tokens, cotangent, back_normed, vectors, *more)


def gelu_tanh(values):
    return jax.nn.gelu(values, approximate=True)


def shampoo(gradient, weight, big, small, big_root, small_root, fan, flipped):
    big_new = beta_stats * big + (1.0 - beta_stats) * lax.dot_general(gradient, gradient, TN, precision=highest)
    small_new = beta_stats * small + (1.0 - beta_stats) * lax.dot_general(gradient, gradient, NT, precision=highest)
    if flipped:
        turned = lax.dot_general(small_root, gradient, TN, precision=highest)
        turned = lax.dot_general(turned, big_root, NT, precision=highest)
    else:
        turned = lax.dot_general(small_root, gradient, NN, precision=highest)
        turned = lax.dot_general(turned, big_root, NN, precision=highest)
    square = jnp.mean(turned * turned)
    weight_new = weight - rate_matrix / math.sqrt(fan) * turned * lax.rsqrt(square + 1e-06)
    return (big_new, small_new, weight_new)


def diagonal_rule(values, moment, gradient):
    moment_new = beta_moment * moment + (1.0 - beta_moment) * gradient * gradient
    return (moment_new, values - rate_vector * gradient / (jnp.sqrt(moment_new) + 1e-08))


def body(
    tokens,
    cotangent,
    lengths,
    orientation,
    joint_weight,
    output_weight,
    expand_weight,
    shrink_weight,
    norm_params,
    expand_bias,
    norm_moment,
    bias_moment,
    joint_left,
    joint_right,
    joint_left_root,
    joint_right_root,
    output_left,
    output_right,
    output_left_root,
    output_right_root,
    expand_left,
    expand_right,
    expand_left_root,
    expand_right_root,
    shrink_left,
    shrink_right,
    shrink_left_root,
    shrink_right_root,
):
    n_mp, n_seq = lax.axis_size("mp"), lax.axis_size("seq")
    mp_index, seq_index = lax.axis_index("mp"), lax.axis_index("seq")
    seqs, local, width = tokens.shape
    rows = seqs * local
    share = norm_params.shape[1]
    per = seqs // n_seq
    paired = n_mp == 2 and per == 2
    flip = mp_index if paired else jnp.zeros((), jnp.int32)
    flip_one = jnp.reshape(flip, (1,)).astype(jnp.int32)

    output_t, shrink_t = output_weight.T, shrink_weight.T
    if paired:
        other_vectors = swap(norm_params, "mp", 1)
        upper = mp_index != 0
        vectors = jnp.concatenate(
            [jnp.where(upper, other_vectors, norm_params), jnp.where(upper, norm_params, other_vectors)], axis=1
        )
    else:
        vectors = lax.all_gather(norm_params, "mp", axis=1, tiled=True)
    joint_full = gather_rows(joint_weight.astype(bf16))
    output_full = gather_rows(output_t.astype(bf16))
    expand_full = gather_rows(expand_weight.astype(bf16))
    shrink_full = gather_rows(shrink_t.astype(bf16))

    def own_share(values):
        return lax.dynamic_slice_in_dim(values, mp_index * share, share, values.ndim - 1)

    def to_whole(values):
        return lax.all_to_all(values, "seq", 0, 0, tiled=True)

    tables = rope_tables()
    normed, normed_own = norm(tokens, vectors, flip_one)
    normed_rows = normed.reshape(rows, width)
    cot_rows = cotangent.reshape(rows, width)
    ids = [flip, 1 - flip] if paired else list(range(per))

    if paired:
        first = to_whole(normed_own).reshape(LEN, width)
        normed_seqs = [first, swap(first, "mp", 1)]
    else:
        split = normed.reshape(n_seq, per, local, width)
        normed_seqs = [to_whole(split[:, t]).reshape(LEN, width) for t in range(per)]
    back_context = mm(cot_rows, output_full).astype(bf16).reshape(n_seq, per, local, -1)
    part = back_context.shape[-1]

    contexts, grads = [], []
    for t, which in enumerate(ids):
        back_one = lax.dynamic_index_in_dim(back_context, which, 1, False)
        back_one = to_whole(back_one).reshape(LEN, part)
        spot = seq_index * per + which
        info = jnp.stack(
            [lax.dynamic_index_in_dim(lengths, spot, 0, False), lax.dynamic_index_in_dim(orientation, spot, 0, False)]
        )
        joint_rows = project(normed_seqs[t], joint_full, tables)
        context_one, grad_one = attend(info, joint_rows, back_one, tables)
        contexts.append(to_whole(context_one.reshape(n_seq, local, part)))
        grads.append(grad_one)

    pre_act = mm(normed_rows, expand_full) + expand_bias
    active, gelu_back = jax.vjp(gelu_tanh, pre_act)
    active_low = active.astype(bf16)
    grad_pre = gelu_back(mm(cot_rows, shrink_full))[0].astype(bf16)
    bias_term = jnp.sum(grad_pre.astype(f32), 0)
    back_ffn = mm(grad_pre, expand_full, NT).astype(bf16).reshape(n_seq, per, local, width)

    if paired:
        first_even = flip == 0
        context = jnp.stack(
            [jnp.where(first_even, contexts[0], contexts[1]), jnp.where(first_even, contexts[1], contexts[0])], axis=1
        )
    else:
        context = jnp.stack(contexts, axis=1)
    context = context.reshape(rows, part)
    branch = mm(context, output_full, NT) + mm(active_low, shrink_full, NT)
    branch = branch.reshape(seqs, local, width)
    if paired:
        away = lax.dynamic_slice_in_dim(branch, (1 - mp_index) * share, share, 2)
        summed = own_share(branch) + swap(away.astype(bf16), "mp", 1).astype(f32)
    else:
        summed = lax.psum_scatter(branch, "mp", scatter_dimension=2, tiled=True)
    block_output = (own_share(tokens).astype(f32) + summed + norm_params[2]).astype(bf16)

    back_seqs = [mm(grad_one, joint_full, NT) for grad_one in grads]
    cot_sum = None
    if paired:
        back_own = back_seqs[0] + swap(back_seqs[1].astype(bf16), "mp", 1).astype(f32)
        back_own = to_whole(back_own.astype(bf16).reshape(n_seq, local, width))
        ffn_own = lax.dynamic_index_in_dim(back_ffn, flip, 1, False)
        ffn_away = lax.dynamic_index_in_dim(back_ffn, 1 - flip, 1, False)
        total = (ffn_own.astype(f32) + swap(ffn_away, "mp", 1).astype(f32) + back_own.astype(f32)).astype(bf16)
        total_other = swap(total, "mp", 1)
        order = jnp.arange(n_seq, dtype=jnp.int32) * 2
        partial_grad, sums = norm_back(order + flip, tokens, cotangent, total, vectors)
        input_grad, sums_other = norm_back(order + 1 - flip, tokens, cotangent, total_other, vectors, partial_grad)
        sums = sums + sums_other
    else:
        pieces = [lax.psum(one, "mp") for one in back_seqs]
        pieces = [to_whole(one.astype(bf16).reshape(n_seq, local, width)) for one in pieces]
        total = jnp.stack(pieces, axis=1).astype(f32) + lax.psum(back_ffn.astype(f32), "mp")
        total = total.astype(bf16).reshape(seqs, local, width)
        input_grad, sums = norm_back(jnp.arange(seqs, dtype=jnp.int32), tokens, cotangent, total, vectors)

    joint_term = mm(normed_seqs[0], grads[0], TN)
    for one, grad_one in zip(normed_seqs[1:], grads[1:]):
        joint_term = joint_term + mm(one, grad_one, TN)
    expand_term = mm(normed_rows, grad_pre, TN)
    output_term = mm(cot_rows, context, TN)
    shrink_term = mm(cot_rows, active_low, TN)
    expand_grad = scatter_rows(expand_term)
    shrink_grad = scatter_rows(shrink_term)
    joint_grad = scatter_rows(joint_term)
    output_grad = scatter_rows(output_term)
    norm_grad = sum_all(own_share(sums[:3]), ("dp", "seq"))
    bias_grad = sum_all(bias_term, ("dp", "seq"))

    fans = (width, width // 32, width, 4 * width)
    joint_right_new, joint_left_new, joint_new = shampoo(
        joint_grad, joint_weight, joint_right, joint_left, joint_right_root, joint_left_root, fans[0], False
    )
    output_left_new, output_right_new, output_new = shampoo(
        output_grad, output_t, output_left, output_right, output_left_root, output_right_root, fans[1], True
    )
    expand_right_new, expand_left_new, expand_new = shampoo(
        expand_grad, expand_weight, expand_right, expand_left, expand_right_root, expand_left_root, fans[2], False
    )
    shrink_left_new, shrink_right_new, shrink_new = shampoo(
        shrink_grad, shrink_t, shrink_left, shrink_right, shrink_left_root, shrink_right_root, fans[3], True
    )
    norm_moment_new, norm_params_new = diagonal_rule(norm_params, norm_moment, norm_grad)
    bias_moment_new, bias_new = diagonal_rule(expand_bias, bias_moment, bias_grad)
    return (
        block_output,
        input_grad,
        joint_grad,
        output_grad.T,
        expand_grad,
        shrink_grad.T,
        norm_grad,
        bias_grad,
        joint_left_new,
        joint_right_new,
        output_left_new,
        output_right_new,
        expand_left_new,
        expand_right_new,
        shrink_left_new,
        shrink_right_new,
        joint_new,
        output_new.T,
        expand_new,
        shrink_new.T,
        norm_moment_new,
        bias_moment_new,
        norm_params_new,
        bias_new,
    )


def solution(mesh):
    data = P("dp", "seq", None)
    rows = P(("dp", "seq"), "mp")
    cols = P("mp", ("dp", "seq"))
    vector = P(None, "mp")
    placed = (data, data, P("dp"), P("dp"), rows, cols, rows, cols, vector, P("mp"), vector, P("mp")) + (rows,) * 16
    out_placed = (
        (P("dp", "seq", "mp"), data, rows, cols, rows, cols, vector, P("mp"))
        + (rows,) * 8
        + (rows, cols, rows, cols, vector, P("mp"), vector, P("mp"))
    )
    return jax.shard_map(body, mesh=mesh, in_specs=placed, out_specs=out_placed, check_vma=False)
```

```python
import functools
import math

import jax
import jax.numpy as jnp
from jax import lax
from jax.experimental import pallas as pl
from jax.experimental.pallas import tpu as pltpu
from jax.sharding import PartitionSpec as P

HS = 64
ROT = 32
LEN = 1024
BLOCK = 256
CHUNK = 1024
STRIP = 512

norm_eps = 1e-05
beta_stats = 0.95
beta_moment = 0.95
rate_matrix = 0.5
rate_vector = 0.03
bf16 = jnp.bfloat16
f32 = jnp.float32
NT = (((1,), (1,)), ((), ()))
TN = (((0,), (0,)), ((), ()))
NN = (((1,), (0,)), ((), ()))
anywhere = pl.BlockSpec(memory_space=pl.ANY)


def mm(a, b, dims=NN):
    return lax.dot_general(a, b, dims, preferred_element_type=f32)


def bits_of(size):
    return [1 << i for i in range(size.bit_length() - 1)]


def swap(value, axis, bit):
    size = lax.axis_size(axis)
    return lax.ppermute(value, axis, [(i, i ^ bit) for i in range(size)])


def tie(*values):
    return lax.optimization_barrier(values)


def beside(outs, *groups):
    flat = list(outs)
    for group in groups:
        flat += group if isinstance(group, list) else [group]
    flat = list(tie(*flat))
    outs, flat = flat[: len(outs)], flat[len(outs) :]
    result = []
    for group in groups:
        count = len(group) if isinstance(group, list) else 1
        result.append(flat[:count] if isinstance(group, list) else flat[0])
        flat = flat[count:]
    return outs, result


class Gather:
    def __init__(self, shard):
        self.shape = shard.shape
        self.value = shard.reshape((1, 1) + shard.shape)
        self.todo = [("seq", bit) for bit in reversed(bits_of(lax.axis_size("seq")))]
        self.todo += [("dp", bit) for bit in reversed(bits_of(lax.axis_size("dp")))]
        self.pieces = None
        self.order = [0]

    def step(self):
        axis, bit = self.todo.pop(0)
        if axis == "seq":
            mine, other = self.value, swap(self.value, "seq", bit)
            upper = (lax.axis_index("seq") & bit) != 0
            value = jnp.stack([jnp.where(upper, other, mine), jnp.where(upper, mine, other)], axis=1)
            self.value = value.reshape((-1, 1) + self.shape)
            return
        if self.pieces is None:
            self.pieces = [self.value.reshape(-1, self.shape[1])]
        self.pieces = self.pieces + [swap(piece, "dp", bit) for piece in self.pieces]
        self.order = self.order + [r ^ bit for r in self.order]
        if not self.todo:
            self.pieces = [piece for _, piece in sorted(zip(self.order, self.pieces), key=lambda item: item[0])]


def merge_pieces(pieces):
    index = lax.axis_index("dp")
    for bit in bits_of(len(pieces)):
        upper = (index & bit) != 0
        pieces = [jnp.where(upper, pieces[r ^ bit], pieces[r]) for r in range(len(pieces))]
    return jnp.concatenate(pieces, axis=0)


class Scatter:
    def __init__(self, mine, theirs):
        n_dp, n_seq = lax.axis_size("dp"), lax.axis_size("seq")
        self.cols = mine.shape[1]
        self.terms, self.away = [mine], theirs
        self.now = ("dp", 1)
        self.todo = [("dp", bit) for bit in reversed(bits_of(n_dp)[1:])]
        self.todo += [("seq", bit) for bit in bits_of(n_seq)]

    def step(self):
        if self.away is None:
            self.now = self.todo.pop(0)
            rows = self.terms[0].shape[0] // 2
            self.away = sum(term[rows:].astype(f32) for term in self.terms).astype(bf16)
            self.terms = [term[:rows] for term in self.terms]
        self.sent = self.away
        self.terms = self.terms + [swap(self.away, *self.now)]
        self.away = None

    def finish(self):
        while self.todo or self.away is not None:
            self.step()
        return sum(term.astype(f32) for term in self.terms)


def owner_rows(info_ref, dp_half, seq, other, rows):
    block = (info_ref[1] ^ (2 * dp_half + other)) * lax.axis_size("seq") + (info_ref[3] ^ seq)
    return pl.ds(pl.multiple_of(block * rows, rows), rows)


def seq_order():
    order = [0]
    for bit in reversed(bits_of(lax.axis_size("seq"))):
        order = order + [place | bit for place in order]
    return order


def owner_blocks():
    return [(dp_half, seq) for dp_half in range(lax.axis_size("dp") // 2) for seq in seq_order()]


def call(kernel, name, grid, prefetch, ins, outs, us, scratch=(), deps=(), alias=None):
    count = len(prefetch) + len(ins)

    def run(*refs):
        kernel(*refs[:count], *refs[count + len(deps) :])

    return pl.pallas_call(
        run,
        grid_spec=pltpu.PrefetchScalarGridSpec(
            num_scalar_prefetch=len(prefetch),
            grid=grid,
            in_specs=[spec for _, spec in ins] + [anywhere] * len(deps),
            out_specs=[spec for _, spec in outs],
            scratch_shapes=list(scratch),
        ),
        out_shape=[jax.ShapeDtypeStruct(shape, kind) for (shape, kind), _ in outs],
        input_output_aliases=alias or {},
        compiler_params=pltpu.CompilerParams(vmem_limit_bytes=60 * 2**20),
        cost_estimate=pl.CostEstimate(flops=int(us * 0.3e9), bytes_accessed=0, transcendentals=0),
        name=name,
    )(*prefetch, *[array for array, _ in ins], *deps)


def whole(shape):
    return pl.BlockSpec(shape, lambda i, *s: (0,) * len(shape))


def load_pieces(dp_index, piece_refs, full_ref, sem):
    rows = piece_refs[0].shape[0]
    copies = []
    for r, piece in enumerate(piece_refs):
        spot = pl.multiple_of((dp_index ^ r) * rows, rows)
        if piece.shape[1] > full_ref.shape[1]:
            piece = piece.at[:, pl.ds(0, full_ref.shape[1])]
        copies.append(pltpu.make_async_copy(piece, full_ref.at[pl.ds(spot, rows)], sem.at[r]))
    for copy in copies:
        copy.start()
    return copies


def rope_tables():
    lane = jnp.arange(128, dtype=jnp.int32) % HS
    pair = (lane // 2).astype(f32)
    frequency = 10000.0 ** (-2.0 * pair / ROT)
    angles = jnp.arange(LEN, dtype=f32)[:, None] * frequency[None, :]
    turned = (lane < ROT)[None, :]
    cosine = jnp.where(turned, jnp.cos(angles), 1.0)
    sine = jnp.sin(angles)
    to_even = jnp.where(turned & (lane % 2 == 0)[None, :], -sine, 0.0)
    to_odd = jnp.where(turned & (lane % 2 == 1)[None, :], sine, 0.0)
    return cosine, to_even, to_odd


def turn(value, cosine, to_even, to_odd):
    return value * cosine + pltpu.roll(value, 127, 1) * to_even + pltpu.roll(value, 1, 1) * to_odd


def attend_kernel(pieces, info_ref, x_ref, back_ref, c_ref, e_ref, o_ref, *rest):
    piece_refs, rest = rest[:pieces], rest[pieces:]
    ctx_ref, grad_ref, out_ref, w_ref, joint_ref, dk_ref, dv_ref, sem = rest
    part = grad_ref.shape[1] // 3
    pair = pl.program_id(0)
    length, reverse = info_ref[0], info_ref[1]
    lane = lax.broadcasted_iota(jnp.int32, (1, 128), 1)
    zero = jnp.zeros((), bf16)

    @pl.when(pair == 0)
    def _():
        for copy in load_pieces(info_ref[2], piece_refs, w_ref, sem):
            copy.wait()

        def step(i, _):
            rows = pl.ds(pl.multiple_of(i * BLOCK, BLOCK), BLOCK)
            values = mm(x_ref[rows, :], w_ref[...])
            for at in range(0, 3 * part, 128):
                piece = values[:, at : at + 128]
                if at < 2 * part:
                    piece = turn(piece, c_ref[rows, :], e_ref[rows, :], o_ref[rows, :])
                joint_ref[rows, at : at + 128] = piece.astype(bf16)
            return 0

        lax.fori_loop(0, LEN // BLOCK, step, 0)

    q_at, k_at, v_at = (pl.ds(pl.multiple_of(g * part + pair * 128, 128), 128) for g in range(3))
    keys, values = joint_ref[:, k_at], joint_ref[:, v_at]
    key_heads, value_heads = [], []
    for head in range(2):
        inside = (lane // HS) == head
        key_heads.append(jnp.where(inside, keys, zero))
        value_heads.append(jnp.where(inside, values, zero))
    dk_ref[...] = jnp.zeros_like(dk_ref)
    dv_ref[...] = jnp.zeros_like(dv_ref)
    low = jnp.where(reverse == 0, 0, LEN - length)
    high = jnp.where(reverse == 0, length, LEN)
    q_id = lax.broadcasted_iota(jnp.int32, (BLOCK, BLOCK), 0)
    k_id = lax.broadcasted_iota(jnp.int32, (BLOCK, BLOCK), 1)

    def key_bias(start, size):
        spot = start + lax.broadcasted_iota(jnp.int32, (1, size), 1)
        return jnp.where((spot >= low) & (spot < high), 0.0, -1e30)

    def before(block, head):
        begin = block * BLOCK
        stop = begin + BLOCK
        rows = pl.ds(begin, BLOCK)
        inside = (lane // HS) == head
        query = joint_ref[rows, q_at] * jnp.asarray(1.0 / math.sqrt(HS), bf16)
        back = back_ref[rows, :]
        scores = mm(jnp.where(inside, query, zero), keys[:stop], NT)
        at_diag = jnp.where(k_id < q_id, key_bias(begin, BLOCK), jnp.where(k_id == q_id, 0.0, -1e30))
        tail = scores[:, begin:] + at_diag
        scores = jnp.concatenate([scores[:, :begin] + key_bias(0, begin), tail], axis=1) if begin else tail
        back_attend = mm(jnp.where(inside, back, zero), values[:stop], NT)
        return query, back, scores, back_attend

    def between(scores, back_attend):
        top = jnp.max(scores, axis=1, keepdims=True)
        exponent = jnp.exp(scores - top)
        attend = exponent * (1.0 / jnp.sum(exponent, axis=1, keepdims=True))
        delta = jnp.sum(attend * back_attend, axis=1, keepdims=True)
        return attend.astype(bf16), (attend * (back_attend - delta)).astype(bf16)

    kept = {}

    def behind(block, head, query, back, attend_low, grad_scores):
        begin = block * BLOCK
        stop = begin + BLOCK
        rows = pl.ds(begin, BLOCK)
        context = mm(attend_low, value_heads[head][:stop])
        grad_query = mm(grad_scores, key_heads[head][:stop])
        here = slice(head * HS, (head + 1) * HS)
        dk_ref[here, :stop] += mm(query.T[here], grad_scores)
        dv_ref[here, :stop] += mm(back.T[here], attend_low)
        if head == 0:
            kept[block] = context, grad_query
            return
        ctx_ref[rows, :] = (kept[block][0] + context).astype(bf16)
        grad_query = (kept[block][1] + grad_query) * (1.0 / math.sqrt(HS))
        grad_query = turn(grad_query, c_ref[rows, :], -e_ref[rows, :], -o_ref[rows, :])
        grad_ref[rows, q_at] = grad_query.astype(bf16)

    units = [(block, head) for block in range(LEN // BLOCK) for head in range(2)]
    coming, done = before(*units[0]), None
    for number, unit in enumerate(units):
        query, back, scores, back_attend = coming
        if number + 1 < len(units):
            coming = before(*units[number + 1])
        lows = between(scores, back_attend)
        if done is not None:
            behind(*done)
        done = (*unit, query, back, *lows)
    behind(*done)
    grad_key = turn(dk_ref[...].T, c_ref[...], -e_ref[...], -o_ref[...])
    grad_ref[:, k_at] = grad_key.astype(bf16)
    grad_ref[:, v_at] = dv_ref[...].T.astype(bf16)

    @pl.when(pair == pl.num_programs(0) - 1)
    def _():
        def step(i, _):
            rows = pl.ds(pl.multiple_of(i * BLOCK, BLOCK), BLOCK)
            out_ref[rows, :] = mm(grad_ref[rows, :], w_ref[...], NT).astype(out_ref.dtype)
            return 0

        lax.fori_loop(0, LEN // BLOCK, step, 0)


def attend(info, rows, pieces, back_rows, tables, kind, deps):
    width, part = rows.shape[1], back_rows.shape[1]
    cols = 3 * part
    column = pl.BlockSpec((LEN, 128), lambda i, s: (0, i))
    ins = [(rows, whole((LEN, width))), (back_rows, column)]
    ins += [(table, whole((LEN, 128))) for table in tables] + [(piece, anywhere) for piece in pieces]
    outs = [(((LEN, part), bf16), column), (((LEN, cols), bf16), whole((LEN, cols)))]
    outs.append((((LEN, width), kind), whole((LEN, width))))
    scratch = [
        pltpu.VMEM((width, cols), bf16),
        pltpu.VMEM((LEN, cols), bf16),
        pltpu.VMEM((128, LEN), f32),
        pltpu.VMEM((128, LEN), f32),
        pltpu.SemaphoreType.DMA((len(pieces),)),
    ]
    kernel = functools.partial(attend_kernel, len(pieces))
    return call(kernel, "attend", (part // 128,), [info], ins, outs, 40, scratch, deps)


def norm_kernel(info_ref, x_ref, vec_ref, out_ref, own_ref):
    values = x_ref[0].astype(f32)
    centred = values - jnp.mean(values, -1, keepdims=True)
    spread = jnp.mean(centred * centred, -1, keepdims=True)
    normed = centred * lax.rsqrt(spread + norm_eps) * vec_ref[0:1, :] + vec_ref[1:2, :]
    low = normed.astype(bf16)
    out_ref[0] = low

    @pl.when(lax.rem(pl.program_id(0), 2) == info_ref[0])
    def _():
        own_ref[0] = low


def norm(info, tokens, vectors, deps=()):
    seqs, local, width = tokens.shape
    each = pl.BlockSpec((1, local, width), lambda i, s: (i, 0, 0))
    half = pl.BlockSpec((1, local, width), lambda i, s: (i // 2, 0, 0))
    ins = [(tokens, each), (vectors, whole(vectors.shape))]
    outs = [((tokens.shape, bf16), each), (((seqs // 2, local, width), bf16), half)]
    return call(norm_kernel, "norm", (seqs,), [info], ins, outs, 100, deps=deps)


def norm_back_kernel(count, order_ref, x_ref, cot_ref, vec_ref, *rest):
    back_refs = rest[:count]
    out_ref, sums_ref = rest[-2:]
    values = x_ref[0].astype(f32)
    centred = values - jnp.mean(values, -1, keepdims=True)
    spread = jnp.mean(centred * centred, -1, keepdims=True)
    scale = lax.rsqrt(spread + norm_eps)
    xhat = centred * scale
    back = jnp.concatenate([ref[0] for ref in back_refs], axis=1).astype(f32)
    scaled = back * vec_ref[0:1, :]
    shift = jnp.mean(scaled, -1, keepdims=True)
    slope = jnp.mean(scaled * xhat, -1, keepdims=True)
    cot = cot_ref[0].astype(f32)
    out_ref[0] = cot + (scaled - shift - xhat * slope) * scale

    @pl.when(pl.program_id(0) == 0)
    def _():
        sums_ref[...] = jnp.zeros_like(sums_ref)

    sums_ref[0:1, :] += jnp.sum(back * xhat, 0, keepdims=True)
    sums_ref[1:2, :] += jnp.sum(back, 0, keepdims=True)
    sums_ref[2:3, :] += jnp.sum(cot, 0, keepdims=True)


def norm_back(order, tokens, cotangent, back_normed, vectors, deps=(), earlier=None):
    seqs, local, width = tokens.shape
    count = back_normed[0].shape[0]
    picked = pl.BlockSpec((1, local, width), lambda i, s: (s[i], 0, 0))
    here = lambda one: pl.BlockSpec((1, local, one.shape[2]), lambda i, s: (i, 0, 0))
    ins = [(tokens, picked), (cotangent, picked), (vectors, whole(vectors.shape))]
    ins += [(one, here(one)) for one in back_normed]
    alias = {}
    if earlier is not None:
        alias = {1 + len(ins): 0}
        ins.append((earlier, anywhere))
    outs = [((tokens.shape, f32), picked), (((8, width), f32), whole((8, width)))]
    kernel = functools.partial(norm_back_kernel, len(back_normed))
    return call(kernel, "norm_back", (count,), [order], ins, outs, 7, deps=deps, alias=alias)


def back_context_kernel(info_ref, cot_ref, w_ref, own_ref, away_ref):
    local = own_ref.shape[1]
    values = mm(cot_ref[...].reshape(2 * local, -1), w_ref[...]).astype(bf16)
    even = info_ref[0] == 0
    own_ref[0] = jnp.where(even, values[:local], values[local:])
    away_ref[0] = jnp.where(even, values[local:], values[:local])


def back_context_rows(info, cotangent, weight, deps):
    seqs, local, width = cotangent.shape
    part = weight.shape[1]
    half = pl.BlockSpec((1, local, part), lambda i, s: (i, 0, 0))
    ins = [
        (cotangent, pl.BlockSpec((2, local, width), lambda i, s: (i, 0, 0))),
        (weight, whole(weight.shape)),
    ]
    outs = [(((seqs // 2, local, part), bf16), half)] * 2
    return call(back_context_kernel, "back_context", (seqs // 2,), [info], ins, outs, 6, deps=deps)


def feed_kernel(pieces, earlier, info_ref, x_ref, cot_ref, bias_ref, *rest):
    before, rest = rest[:earlier], rest[earlier:]
    piece_refs, rest = rest[:pieces], rest[pieces:]
    branch_ref, own_ref, away_ref, sums_ref, mine_ref, theirs_ref = rest[:6]
    w_ref, up_grad, down_grad, stage_ref, sem, out_sem = rest[6:]
    step = pl.program_id(0)
    width, hidden = up_grad.shape
    dp_index = info_ref[1]

    @pl.when(step == 0)
    def _():
        copies = load_pieces(dp_index, piece_refs, w_ref, sem)
        up_grad[...] = jnp.zeros_like(up_grad)
        down_grad[...] = jnp.zeros_like(down_grad)
        sums_ref[...] = jnp.zeros_like(sums_ref)
        for copy in copies:
            copy.wait()

    x = x_ref[...].reshape(-1, width)
    cot = cot_ref[...].reshape(-1, width)
    x_turned, cot_turned = x.T, cot.T
    rate = math.sqrt(2.0 / math.pi)
    back = jnp.zeros(x.shape, f32)
    branch = jnp.zeros(x.shape, f32)
    chunk = min(CHUNK, hidden)
    for at in range(0, hidden, chunk):
        cols = slice(at, at + chunk)
        up, down = w_ref[:, cols], w_ref[:, hidden + at : hidden + at + chunk]
        pre = mm(x, up) + bias_ref[:, cols]
        back_active = mm(cot, down)
        square = pre * pre
        bent = jnp.tanh(rate * pre * (1.0 + 0.044715 * square))
        half = 0.5 * (1.0 + bent)
        active = (pre * half).astype(bf16)
        slope = half + 0.5 * pre * (1.0 - bent * bent) * (rate * (1.0 + 3 * 0.044715 * square))
        grad_pre = (back_active * slope).astype(bf16)
        sums_ref[:, cols] += jnp.sum(grad_pre.astype(f32), 0, keepdims=True)
        branch += mm(active, down, NT)
        back += mm(grad_pre, up, NT)
        up_grad[:, cols] += mm(x_turned, grad_pre)
        down_grad[:, cols] += mm(cot_turned, active)
    if earlier:
        branch += before[0][...]
    branch_ref[...] = branch
    local = own_ref.shape[1]
    even = info_ref[0] == 0
    own = jnp.where(even, back[:local], back[local:])
    away = jnp.where(even, back[local:], back[:local])
    if earlier:
        own += before[1][0]
        away += before[2][0]
    own_ref[0] = own.astype(own_ref.dtype)
    away_ref[0] = away.astype(away_ref.dtype)

    @pl.when(step == pl.num_programs(0) - 1)
    def _():
        blocks = owner_blocks()
        rows = width // (2 * len(blocks))
        copies = []
        for number, (dp_half, seq) in enumerate(blocks):
            to = pl.ds(number * rows, rows)
            spot = owner_rows(info_ref, dp_half, seq, 1, rows)
            stage_ref[to, :hidden] = up_grad[spot, :].astype(bf16)
            stage_ref[to, hidden:] = down_grad[spot, :].astype(bf16)
            spot = owner_rows(info_ref, dp_half, seq, 0, rows)
            for side, source in enumerate((up_grad, down_grad)):
                target = mine_ref.at[to, pl.ds(side * hidden, hidden)]
                copies.append(pltpu.make_async_copy(source.at[spot], target, out_sem.at[2 * number + side]))
        copies.append(pltpu.make_async_copy(stage_ref, theirs_ref, out_sem.at[2 * len(blocks)]))
        for copy in copies:
            copy.start()
        for copy in copies:
            copy.wait()


def feed(info, normed, cotangent, bias, weights, before=(), deps=()):
    seqs, local, width = normed.shape
    rows, hidden = weights[0].shape[0], weights[0].shape[1] // 2
    pieces = len(weights)
    pair = pl.BlockSpec((2, local, width), lambda i, s: (i, 0, 0))
    half = pl.BlockSpec((1, local, width), lambda i, s: (i, 0, 0))
    flat = pl.BlockSpec((2 * local, width), lambda i, s: (i, 0))
    term_rows = pieces // 2 * rows
    kind = bf16 if before else f32
    ins = [(normed, pair), (cotangent, pair), (bias, whole((1, hidden)))]
    ins += list(zip(before, [flat, half, half])) + [(piece, anywhere) for piece in weights]
    outs = [
        (((seqs * local, width), f32), flat),
        (((seqs // 2, local, width), kind), half),
        (((seqs // 2, local, width), kind), half),
        (((1, hidden), f32), whole((1, hidden))),
        (((term_rows, 2 * hidden), f32), anywhere),
        (((term_rows, 2 * hidden), bf16), anywhere),
    ]
    scratch = [
        pltpu.VMEM((width, 2 * hidden), bf16),
        pltpu.VMEM((width, hidden), f32),
        pltpu.VMEM((width, hidden), f32),
        pltpu.VMEM((term_rows, 2 * hidden), bf16),
        pltpu.SemaphoreType.DMA((pieces,)),
        pltpu.SemaphoreType.DMA((2 * len(owner_blocks()) + 1,)),
    ]
    kernel = functools.partial(feed_kernel, pieces, len(before))
    return call(kernel, "feed", (seqs // 2,), [info], ins, outs, 37, scratch, deps)


def split_term(info_ref, sum_ref, mine_ref, theirs_ref):
    blocks = owner_blocks()
    rows = sum_ref.shape[0] // (2 * len(blocks))
    for number, (dp_half, seq) in enumerate(blocks):
        to = slice(number * rows, (number + 1) * rows)
        mine_ref[to, :] = sum_ref[owner_rows(info_ref, dp_half, seq, 0, rows), :]
        theirs_ref[to, :] = sum_ref[owner_rows(info_ref, dp_half, seq, 1, rows), :].astype(bf16)


def branch_kernel(last, order_ref, info_ref, context_ref, feed_ref, cot_ref, w_ref, *rest):
    before_ref = rest[0]
    own_ref, away_ref, rest = rest[last], rest[last + 1], rest[last + 2 :]
    step = pl.program_id(0)
    context = context_ref[0]
    share = own_ref.shape[2]
    own = pl.ds(pl.multiple_of(info_ref[2] * share, share), share)
    away = pl.ds(pl.multiple_of((1 - info_ref[2]) * share, share), share)
    own_ref[0] = feed_ref[0, :, own] + mm(context, w_ref[own, :], NT)
    away_ref[0] = (feed_ref[0, :, away] + mm(context, w_ref[away, :], NT)).astype(bf16)
    term = mm(cot_ref[0], context, TN)
    sum_ref = rest[-1]

    @pl.when(step == 0)
    def _():
        sum_ref[...] = term + before_ref[...] if last else term

    @pl.when(step > 0)
    def _():
        sum_ref[...] += term

    if last:

        @pl.when(step == pl.num_programs(0) - 1)
        def _():
            split_term(info_ref, sum_ref, *rest[:2])


def branch_rows(order, info, context, feed_branch, cotangent, weight, deps, before=None):
    count, local, part = context.shape
    width = cotangent.shape[2]
    last = before is not None
    half = pl.BlockSpec((1, local, width // 2), lambda i, s, t: (i, 0, 0))
    picked = pl.BlockSpec((1, local, width), lambda i, s, t: (s[i], 0, 0))
    ins = [(context, pl.BlockSpec((1, local, part), lambda i, s, t: (i, 0, 0)))]
    ins += [(feed_branch, picked), (cotangent, picked), (weight, whole(weight.shape))]
    if last:
        ins.append((before, whole(before.shape)))
    terms = [((width // 2, part), f32), ((width // 2, part), bf16)] if last else [((width, part), f32)]
    outs = [(((count, local, width // 2), kind), half) for kind in (f32, bf16)]
    outs += [(term, whole(term[0])) for term in terms]
    scratch = [pltpu.VMEM((width, part), f32)] * last
    kernel = functools.partial(branch_kernel, int(last))
    return call(kernel, "branch", (count,), [order, info], ins, outs, 9, scratch, deps)


def output_kernel(info_ref, x_ref, own_ref, own_got_ref, other_ref, other_got_ref, vec_ref, out_ref):
    even = info_ref[0] == 0
    own = own_ref[0] + own_got_ref[0].astype(f32)
    other = other_ref[0] + other_got_ref[0].astype(f32)
    total = jnp.concatenate([jnp.where(even, own, other), jnp.where(even, other, own)], axis=0)
    out_ref[...] = (x_ref[...].astype(f32) + total + vec_ref[2:3, :]).astype(bf16)


def output_rows(info, tokens, own, own_got, other, other_got, params_here, deps):
    seqs, local, width = tokens.shape
    share = own.shape[2]
    half = pl.BlockSpec((1, local, share), lambda i, s: (i, 0, 0))
    ins = [(tokens.reshape(-1, width), pl.BlockSpec((2 * local, share), lambda i, s: (i, s[2])))]
    ins += [(one, half) for one in (own, own_got, other, other_got)] + [(params_here, whole(params_here.shape))]
    outs = [(((seqs * local, share), bf16), pl.BlockSpec((2 * local, share), lambda i, s: (i, 0)))]
    return call(output_kernel, "output", (seqs // 2,), [info], ins, outs, 6, deps=deps)[0]


def joint_term_kernel(count, info_ref, *refs):
    xs, grads, (mine_ref, theirs_ref, sum_ref) = refs[:count], refs[count : 2 * count], refs[2 * count :]
    term = mm(xs[0][...], grads[0][...], TN)
    for x, grad in zip(xs[1:], grads[1:]):
        term += mm(x[...], grad[...], TN)
    sum_ref[...] = term
    steps = pl.num_programs(0) // 2
    order = seq_order()
    rows = term.shape[0] // len(order)
    parts = [sum_ref[pl.ds(pl.multiple_of((info_ref[3] ^ seq) * rows, rows), rows), :] for seq in order]

    @pl.when(pl.program_id(0) < steps)
    def _():
        for number, part in enumerate(parts):
            theirs_ref[number * rows : (number + 1) * rows, :] = part.astype(bf16)

    @pl.when(pl.program_id(0) >= steps)
    def _():
        for number, part in enumerate(parts):
            mine_ref[number * rows : (number + 1) * rows, :] = part


def joint_term(info, xs, grads, deps):
    pieces = lax.axis_size("dp")
    steps = pieces // 2
    width, cols = xs[0].shape[1], grads[0].shape[1]
    rows = width // pieces

    def picked(i, s):
        return (0, s[1] ^ (2 * lax.rem(i, steps) + 1 - i // steps))

    ins = [(x, pl.BlockSpec((LEN, rows), picked)) for x in xs] + [(grad, whole((LEN, cols))) for grad in grads]
    outs = [
        (((steps * rows, cols), f32), pl.BlockSpec((rows, cols), lambda i, s: (jnp.maximum(i - steps, 0), 0))),
        (((steps * rows, cols), bf16), pl.BlockSpec((rows, cols), lambda i, s: (jnp.minimum(i, steps - 1), 0))),
    ]
    scratch = [pltpu.VMEM((rows, cols), f32)]
    kernel = functools.partial(joint_term_kernel, len(xs))
    return call(kernel, "joint_term", (pieces,), [info], ins, outs, 12, scratch, deps)


def halves(values):
    high = values.astype(bf16)
    return high, (values - high.astype(f32)).astype(bf16)


def mm3(a, b, dims):
    a_high, a_low = a
    b_high, b_low = b
    return mm(a_high, b_high, dims) + (mm(a_high, b_low, dims) + mm(a_low, b_high, dims))


def shampoo_kernel(fan, flipped, g_ref, w_ref, big_ref, small_ref, root_ref, small_root_ref, *rest):
    big_out, small_out, w_out, left_ref, right_ref, sg_ref, turned_ref = rest
    step = pl.program_id(0)
    rows, block = g_ref.shape[0], big_ref.shape[0]
    cols = pl.ds(pl.multiple_of(step * block, block), block)

    @pl.when(step == 0)
    def _():
        g = halves(g_ref[...])
        left_ref[...] = jnp.concatenate([g[0], g[1], g[0]], axis=0)
        right_ref[...] = jnp.concatenate([g[0], g[0], g[1]], axis=0)
        turned = mm3(halves(small_root_ref[...]), g, TN if flipped else NN)
        sg_ref[...] = jnp.concatenate(halves(turned), axis=0)
        small_out[...] = beta_stats * small_ref[...] + (1.0 - beta_stats) * mm3(g, g, NT)

    big_out[...] = beta_stats * big_ref[...] + (1.0 - beta_stats) * mm(left_ref[:, cols], right_ref[...], TN)
    root_high, root_low = halves(root_ref[...])
    if flipped:
        both = mm(sg_ref[...], root_high, NT)
        turned_ref[:, cols] = both[:rows] + both[rows:] + mm(sg_ref[:rows, :], root_low, NT)
    else:
        both = mm(sg_ref[:, cols], root_high)
        part = both[:rows] + both[rows:] + mm(sg_ref[:rows, cols], root_low)

        @pl.when(step == 0)
        def _():
            turned_ref[...] = part

        @pl.when(step > 0)
        def _():
            turned_ref[...] += part

    @pl.when(step == pl.num_programs(0) - 1)
    def _():
        turned = turned_ref[...]
        square = jnp.sum(turned * turned, axis=(0, 1), keepdims=True) * (1.0 / turned.size)
        w_out[...] = w_ref[...] - rate_matrix / math.sqrt(fan) * turned * lax.rsqrt(square + 1e-06)


def shampoo(gradient, weight, big, small, big_root, small_root, fan, flipped, deps=()):
    rows, size = gradient.shape
    block = min(STRIP, size)
    if size % block:
        block = size
    strip = pl.BlockSpec((block, size), lambda i: (i, 0))
    square = whole((rows, rows))
    flat = whole((rows, size))
    ins = [(gradient, flat), (weight, flat), (big, strip), (small, square), (big_root, strip), (small_root, square)]
    outs = [(((size, size), f32), strip), (((rows, rows), f32), square), (((rows, size), f32), flat)]
    scratch = [
        pltpu.VMEM((3 * rows, size), bf16),
        pltpu.VMEM((3 * rows, size), bf16),
        pltpu.VMEM((2 * rows, size), bf16),
        pltpu.VMEM((rows, size), f32),
    ]
    kernel = functools.partial(shampoo_kernel, fan, flipped)
    return call(kernel, "shampoo", (size // block,), [], ins, outs, 19 * size * size / 2048**2, scratch, deps)


def diagonal_rule(values, moment, gradient):
    moment_new = beta_moment * moment + (1.0 - beta_moment) * gradient * gradient
    return (moment_new, values - rate_vector * gradient / (jnp.sqrt(moment_new) + 1e-08))


def body(
    tokens,
    cotangent,
    lengths,
    orientation,
    joint_weight,
    output_weight,
    expand_weight,
    shrink_weight,
    norm_params,
    expand_bias,
    norm_moment,
    bias_moment,
    joint_left,
    joint_right,
    joint_left_root,
    joint_right_root,
    output_left,
    output_right,
    output_left_root,
    output_right_root,
    expand_left,
    expand_right,
    expand_left_root,
    expand_right_root,
    shrink_left,
    shrink_right,
    shrink_left_root,
    shrink_right_root,
):
    n_mp, n_seq, n_dp = lax.axis_size("mp"), lax.axis_size("seq"), lax.axis_size("dp")
    mp_index, seq_index, dp_index = lax.axis_index("mp"), lax.axis_index("seq"), lax.axis_index("dp")
    seqs, local, width = tokens.shape
    rows = seqs * local
    share = norm_params.shape[1]
    per = seqs // n_seq
    paired = n_mp == 2 and per == 2
    flip = mp_index if paired else jnp.zeros((), jnp.int32)
    info = jnp.stack([flip, dp_index, mp_index, seq_index]).astype(jnp.int32)
    ids = [1 - flip, flip] if paired else list(range(per))

    def facts(which):
        spot = seq_index * per + which
        values = [lax.dynamic_index_in_dim(one, spot, 0, False) for one in (lengths, orientation)]
        return jnp.stack(values + [dp_index])

    def own_share(values):
        return lax.dynamic_slice_in_dim(values, mp_index * share, share, values.ndim - 1)

    def to_whole(values):
        return lax.all_to_all(values, "seq", 0, 0, tiled=True)

    output_t, shrink_t = output_weight.T, shrink_weight.T
    hidden = expand_weight.shape[1]
    half = hidden // 2
    both = lambda left, right: jnp.concatenate([left.astype(bf16), right.astype(bf16)], axis=1)
    early = Gather(both(expand_weight[:, :half], shrink_t[:, :half]))
    middle = Gather(both(joint_weight, output_t))
    late = Gather(both(expand_weight[:, half:], shrink_t[:, half:]))
    along = len(bits_of(n_seq))

    early.value, params_here = tie(early.value, norm_params)
    if paired:
        other_params = swap(params_here, "mp", 1)
        upper = mp_index != 0
        vectors = jnp.concatenate(
            [jnp.where(upper, other_params, norm_params), jnp.where(upper, norm_params, other_params)], axis=1
        )
    else:
        vectors = lax.all_gather(params_here, "mp", axis=1, tiled=True)
    tables = rope_tables()
    facts_of = [facts(which) for which in ids]
    normed, normed_own = norm(info, tokens, vectors)
    early.step()
    early.value, middle.value, late.value, normed, normed_own = tie(
        early.value, middle.value, late.value, normed, normed_own
    )
    for _ in range(1, along):
        early.step()
    middle.step()
    early.value, middle.value, late.value = tie(early.value, middle.value, late.value)
    for _ in range(1, along):
        middle.step()
    late.step()
    while len(early.todo) > 1:
        early.step()
    (middle.value, late.value, normed_own), (early.pieces,) = beside(
        [middle.value, late.value, normed_own], early.pieces
    )
    early.step()
    while len(middle.todo) > 1:
        middle.step()
    for _ in range(1, along):
        late.step()
    (late.value, normed_own), (early.pieces, tables, facts_of) = beside(
        [late.value, normed_own], early.pieces, list(tables), facts_of
    )
    while len(late.todo) > 1:
        late.step()

    if paired:
        arrived = [to_whole(normed_own).reshape(LEN, width)]
    else:
        split = normed.reshape(n_seq, per, local, width)
        arrived = [to_whole(split[:, t]).reshape(LEN, width) for t in range(per)]

    first = feed(info, normed, cotangent, expand_bias[None, :half], early.pieces, deps=[late.pieces[0]])
    first, (middle.pieces, late.pieces) = beside(first, middle.pieces, late.pieces)
    middle.step()
    late.step()
    scatter_early = Scatter(first[4], first[5])
    scatter_early.step()
    normed_seqs = [swap(arrived[0], "mp", 1), arrived[0]] if paired else arrived
    joint_cols = joint_weight.shape[1]
    output_full = merge_pieces([piece[:, joint_cols:] for piece in middle.pieces])
    part = output_full.shape[1]
    back_parts = back_context_rows(info, cotangent, output_full, [])
    back_parts, (late.pieces, scatter_early.terms[-1], arrived) = beside(
        back_parts, late.pieces, scatter_early.terms[-1], arrived
    )
    if paired:
        normed_seqs[1] = arrived[0]
        back_parts = back_parts[::-1]
    back_whole = [to_whole(back_parts[0]).reshape(LEN, part)]
    scatter_early.step()
    second = feed(info, normed, cotangent, expand_bias[None, half:], late.pieces, first[:3])
    second, (normed_seqs, back_whole, scatter_early.terms[-1]) = beside(
        second, normed_seqs, back_whole, scatter_early.terms[-1]
    )
    feed_branch, ffn_own, ffn_away = second[:3]
    bias_term = jnp.concatenate([first[3][0], second[3][0]])

    fans = (width, width // 32, width, 4 * width)
    expand_state = (expand_weight, expand_right, expand_left, expand_right_root, expand_left_root, fans[2], False)
    shrink_state = (shrink_t, shrink_left, shrink_right, shrink_left_root, shrink_right_root, fans[3], True)
    joint_state = (joint_weight, joint_right, joint_left, joint_right_root, joint_left_root, fans[0], False)
    output_state = (output_t, output_left, output_right, output_left_root, output_right_root, fans[1], True)
    kind = bf16 if paired else f32
    scatter_late = Scatter(second[4], second[5])
    scatter_late.step()
    ffn_got = [swap(ffn_away, "mp", 1)] if paired else []
    back_whole.append(to_whole(back_parts[1]).reshape(LEN, part))
    scatter_early.step()
    scatter_late.step()
    attended = attend(facts_of[0], normed_seqs[0], middle.pieces, back_whole[0], tables, kind, [])
    attended, (ffn_got, back_late, scatter_early.terms[-1], scatter_late.terms[-1]) = beside(
        attended, ffn_got, back_whole[1], scatter_early.terms[-1], scatter_late.terms[-1]
    )
    context_other, grad_other, back_other = attended
    received = [swap(back_other, "mp", 1)] if paired else []
    context_other = to_whole(context_other.reshape(n_seq, local, part))
    scatter_early.step()
    scatter_late.step()
    attended = attend(facts_of[1], normed_seqs[1], middle.pieces, back_late, tables, kind, [])
    attended, (received, context_other, scatter_early.terms[-1], scatter_late.terms[-1]) = beside(
        attended, received, context_other, scatter_early.terms[-1], scatter_late.terms[-1]
    )
    context_own, grad_own, back_own = attended
    context_own = context_own.reshape(n_seq, local, part)
    grads = [grad_other, grad_own]

    def feed_grads():
        early_grad, late_grad = scatter_early.finish(), scatter_late.finish()
        expand_grad = jnp.concatenate([early_grad[:, :half], late_grad[:, :half]], axis=1)
        return expand_grad, jnp.concatenate([early_grad[:, half:], late_grad[:, half:]], axis=1)

    if paired:
        order = jnp.arange(n_seq, dtype=jnp.int32) * 2
        own_order, other_order = order + flip, order + 1 - flip
        back_sum = (back_own.astype(f32) + received[0].astype(f32)).astype(bf16)
        scatter_late.step()
        branch_in = feed_branch.reshape(tokens.shape)
        branched = branch_rows(other_order, info, context_other, branch_in, cotangent, output_full, [back_sum])
        branched, (back_sum, context_own, scatter_late.terms[-1]) = beside(
            branched, back_sum, context_own, scatter_late.terms[-1]
        )
        other_own, other_away, output_term = branched
        own_got = swap(other_away, "mp", 1)
        context_own = to_whole(context_own)
        joint_parts = joint_term(info, normed_seqs, grads, [scatter_late.terms[-1]])
        joint_parts, (context_own, back_sum) = beside(joint_parts, context_own, back_sum)
        back_sum = to_whole(back_sum.reshape(n_seq, local, width))
        scatter_joint = Scatter(*joint_parts)
        scatter_joint.step()
        expand_grad, shrink_grad = feed_grads()
        expand_new = shampoo(expand_grad, *expand_state, [joint_parts[0]])
        expand_new, (scatter_joint.terms[-1], own_got) = beside(expand_new, scatter_joint.terms[-1], own_got)
        scatter_joint.step()
        branched = branch_rows(
            own_order, info, context_own, branch_in, cotangent, output_full, [expand_new[1]], output_term
        )
        own_own, own_away, output_mine, output_theirs = branched
        other_got = swap(own_away, "mp", 1)
        scatter_output = Scatter(output_mine, output_theirs)
        scatter_output.step()
        shrink_new = shampoo(shrink_grad, *shrink_state, [output_mine])
        shrink_new, (back_sum, scatter_joint.terms[-1], scatter_output.terms[-1]) = beside(
            shrink_new, back_sum, scatter_joint.terms[-1], scatter_output.terms[-1]
        )
        scatter_joint.step()
        scatter_output.step()
        total = ffn_own.astype(f32) + ffn_got[0].astype(f32) + back_sum.astype(f32)
        total = total.astype(bf16)
        total_other = swap(total, "mp", 1)
        backed = norm_back(own_order, tokens, cotangent, [total], vectors, [shrink_new[1]])
        backed, (scatter_joint.terms[-1], scatter_output.terms[-1], other_got) = beside(
            backed, scatter_joint.terms[-1], scatter_output.terms[-1], other_got
        )
        input_grad, sums = backed
        scatter_joint.step()
        scatter_output.step()
        hops = [(axis, bit) for axis in ("dp", "seq") for bit in bits_of(lax.axis_size(axis))]
        vector_terms = jnp.concatenate([sums[:3].reshape(-1), bias_term])
        vector_got = swap(vector_terms, *hops[0])
        block_output = output_rows(
            info, tokens, own_own, own_got, other_own, other_got, norm_params, [sums]
        )
        (block_output,), (scatter_joint.terms[-1], scatter_output.terms[-1], vector_got) = beside(
            [block_output], scatter_joint.terms[-1], scatter_output.terms[-1], vector_got
        )
        block_output = block_output.reshape(seqs, local, share)
        vector_terms = vector_terms + vector_got
        vector_got = swap(vector_terms, *hops[1])
        joint_grad = scatter_joint.finish()
        scatter_output.step()
        joint_new = shampoo(joint_grad, *joint_state, [block_output])
        joint_new, (scatter_output.terms[-1], vector_got) = beside(
            joint_new, scatter_output.terms[-1], vector_got
        )
        vector_terms = vector_terms + vector_got
        vector_got = swap(vector_terms, *hops[2])
        output_grad = scatter_output.finish()
        output_new = shampoo(output_grad, *output_state, [joint_new[1]])
        output_new, (total_other, vector_got) = beside(output_new, total_other, vector_got)
        vector_terms = vector_terms + vector_got
        vector_got = swap(vector_terms, *hops[3])
        backed = norm_back(other_order, tokens, cotangent, [total_other], vectors, [], input_grad)
        backed, (vector_got,) = beside(backed, vector_got)
        input_grad = backed[0]
        vector_terms = vector_terms + vector_got
        for hop in hops[4:]:
            vector_terms = vector_terms + swap(vector_terms, *hop)
        sums, bias_term = vector_terms[: 3 * width].reshape(3, width), vector_terms[3 * width :]
        away_share = lax.dynamic_slice_in_dim(sums, (1 - mp_index) * share, share, 1)
        sums = own_share(sums) + swap(away_share, "mp", 1)
        vector_terms = jnp.concatenate([sums.reshape(-1), bias_term])
    else:
        context_own = to_whole(context_own)
        context = jnp.stack([context_other, context_own], axis=1).reshape(rows, part)
        branch = feed_branch + mm(context, output_full, NT)
        summed = lax.psum_scatter(branch, "mp", scatter_dimension=1, tiled=True).reshape(seqs, local, share)
        block_output = (own_share(tokens).astype(f32) + summed + norm_params[2]).astype(bf16)
        output_term = mm(cotangent.reshape(rows, width), context, TN).reshape(n_dp, n_seq, -1, part)
        pick = lambda dp_half, seq, other: output_term[dp_index ^ (2 * dp_half + other), seq_index ^ seq]
        output_mine, output_theirs = (
            jnp.concatenate([pick(*block, other) for block in owner_blocks()]) for other in (0, 1)
        )
        back = [lax.psum(one, "mp") for one in (back_other, back_own)]
        back = [to_whole(one.astype(bf16).reshape(n_seq, local, width)) for one in back]
        feed_back = jnp.stack([ffn_own, ffn_away], axis=1).astype(f32)
        total = jnp.stack(back, axis=1).astype(f32) + lax.psum(feed_back, "mp")
        total = total.astype(bf16).reshape(seqs, local, width)
        input_grad, sums = norm_back(jnp.arange(seqs, dtype=jnp.int32), tokens, cotangent, [total], vectors)
        sums = own_share(sums[:3])
        joint_grad = Scatter(*joint_term(info, normed_seqs, grads, [])).finish()
        output_grad = Scatter(output_mine, output_theirs.astype(bf16)).finish()
        expand_grad, shrink_grad = feed_grads()
        expand_new = shampoo(expand_grad, *expand_state)
        shrink_new = shampoo(shrink_grad, *shrink_state)
        joint_new = shampoo(joint_grad, *joint_state)
        output_new = shampoo(output_grad, *output_state)
        vector_terms = jnp.concatenate([sums.reshape(-1), bias_term])
        for axis in ("dp", "seq"):
            for bit in bits_of(lax.axis_size(axis)):
                vector_terms = vector_terms + swap(vector_terms, axis, bit)

    norm_grad, bias_grad = vector_terms[: 3 * share].reshape(3, share), vector_terms[3 * share :]
    joint_right_new, joint_left_new, joint_new = joint_new
    output_left_new, output_right_new, output_new = output_new
    expand_right_new, expand_left_new, expand_new = expand_new
    shrink_left_new, shrink_right_new, shrink_new = shrink_new
    norm_moment_new, norm_params_new = diagonal_rule(norm_params, norm_moment, norm_grad)
    bias_moment_new, bias_new = diagonal_rule(expand_bias, bias_moment, bias_grad)
    return (
        block_output,
        input_grad,
        joint_grad,
        output_grad.T,
        expand_grad,
        shrink_grad.T,
        norm_grad,
        bias_grad,
        joint_left_new,
        joint_right_new,
        output_left_new,
        output_right_new,
        expand_left_new,
        expand_right_new,
        shrink_left_new,
        shrink_right_new,
        joint_new,
        output_new.T,
        expand_new,
        shrink_new.T,
        norm_moment_new,
        bias_moment_new,
        norm_params_new,
        bias_new,
    )


def solution(mesh):
    data = P("dp", "seq", None)
    rows = P(("dp", "seq"), "mp")
    cols = P("mp", ("dp", "seq"))
    vector = P(None, "mp")
    placed = (data, data, P("dp"), P("dp"), rows, cols, rows, cols, vector, P("mp"), vector, P("mp")) + (rows,) * 16
    out_placed = (
        (P("dp", "seq", "mp"), data, rows, cols, rows, cols, vector, P("mp"))
        + (rows,) * 8
        + (rows, cols, rows, cols, vector, P("mp"), vector, P("mp"))
    )
    return jax.shard_map(body, mesh=mesh, in_specs=placed, out_specs=out_placed, check_vma=False)
```

```python
import functools
import math

import jax
import jax.numpy as jnp
from jax import lax
from jax.experimental import pallas as pl
from jax.experimental.pallas import tpu as pltpu
from jax.sharding import PartitionSpec as P

HS = 64
ROT = 32
LEN = 1024
BLOCK = 256
CHUNK = 1024
STRIP = 512

norm_eps = 1e-05
beta_stats = 0.95
beta_moment = 0.95
rate_matrix = 0.5
rate_vector = 0.03
bf16 = jnp.bfloat16
f32 = jnp.float32
NT = (((1,), (1,)), ((), ()))
TN = (((0,), (0,)), ((), ()))
NN = (((1,), (0,)), ((), ()))
anywhere = pl.BlockSpec(memory_space=pl.ANY)


def mm(a, b, dims=NN):
    return lax.dot_general(a, b, dims, preferred_element_type=f32)


def bits_of(size):
    return [1 << i for i in range(size.bit_length() - 1)]


def swap(value, axis, bit):
    size = lax.axis_size(axis)
    return lax.ppermute(value, axis, [(i, i ^ bit) for i in range(size)])


def tie(*values):
    return lax.optimization_barrier(values)


def beside(outs, *groups):
    flat = list(outs)
    for group in groups:
        flat += group if isinstance(group, list) else [group]
    flat = list(tie(*flat))
    outs, flat = flat[: len(outs)], flat[len(outs) :]
    result = []
    for group in groups:
        count = len(group) if isinstance(group, list) else 1
        result.append(flat[:count] if isinstance(group, list) else flat[0])
        flat = flat[count:]
    return outs, result


class Gather:
    def __init__(self, shard):
        self.shape = shard.shape
        self.value = shard
        self.todo = [("seq", bit) for bit in reversed(bits_of(lax.axis_size("seq")))]
        self.todo += [("dp", bit) for bit in reversed(bits_of(lax.axis_size("dp")))]
        self.pieces = None
        self.order = [0]

    def step(self):
        axis, bit = self.todo.pop(0)
        if axis == "seq":
            rows = self.shape[0]
            mine, other = self.value, swap(self.value, "seq", bit)
            upper = (lax.axis_index("seq") & bit) != 0
            parts = []
            for at in range(0, mine.shape[0], rows):
                one, two = mine[at : at + rows], other[at : at + rows]
                parts += [jnp.where(upper, two, one), jnp.where(upper, one, two)]
            self.value = jnp.concatenate(parts, axis=0)
            return
        if self.pieces is None:
            self.pieces = [self.value]
        self.pieces = self.pieces + [swap(piece, "dp", bit) for piece in self.pieces]
        self.order = self.order + [r ^ bit for r in self.order]
        if not self.todo:
            self.pieces = [piece for _, piece in sorted(zip(self.order, self.pieces), key=lambda item: item[0])]


def merge_pieces(pieces):
    index = lax.axis_index("dp")
    for bit in bits_of(len(pieces)):
        upper = (index & bit) != 0
        pieces = [jnp.where(upper, pieces[r ^ bit], pieces[r]) for r in range(len(pieces))]
    return jnp.concatenate(pieces, axis=0)


class Scatter:
    def __init__(self, mine, theirs):
        n_dp, n_seq = lax.axis_size("dp"), lax.axis_size("seq")
        self.cols = mine.shape[1]
        self.terms, self.away = [mine], theirs
        self.now = ("dp", 1)
        self.todo = [("dp", bit) for bit in reversed(bits_of(n_dp)[1:])]
        self.todo += [("seq", bit) for bit in bits_of(n_seq)]

    def step(self):
        if self.away is None:
            self.now = self.todo.pop(0)
            rows = self.terms[0].shape[0] // 2
            self.away = sum(term[rows:].astype(f32) for term in self.terms).astype(bf16)
            self.terms = [term[:rows] for term in self.terms]
        self.sent = self.away
        self.terms = self.terms + [swap(self.away, *self.now)]
        self.away = None

    def finish(self):
        while self.todo or self.away is not None:
            self.step()
        return sum(term.astype(f32) for term in self.terms)


def owner_rows(info_ref, dp_half, seq, other, rows):
    block = (info_ref[1] ^ (2 * dp_half + other)) * lax.axis_size("seq") + (info_ref[3] ^ seq)
    return pl.ds(pl.multiple_of(block * rows, rows), rows)


def seq_order():
    order = [0]
    for bit in reversed(bits_of(lax.axis_size("seq"))):
        order = order + [place | bit for place in order]
    return order


def owner_blocks():
    return [(dp_half, seq) for dp_half in range(lax.axis_size("dp") // 2) for seq in seq_order()]


def call(kernel, name, grid, prefetch, ins, outs, us, scratch=(), deps=(), alias=None):
    count = len(prefetch) + len(ins)

    def run(*refs):
        kernel(*refs[:count], *refs[count + len(deps) :])

    return pl.pallas_call(
        run,
        grid_spec=pltpu.PrefetchScalarGridSpec(
            num_scalar_prefetch=len(prefetch),
            grid=grid,
            in_specs=[spec for _, spec in ins] + [anywhere] * len(deps),
            out_specs=[spec for _, spec in outs],
            scratch_shapes=list(scratch),
        ),
        out_shape=[jax.ShapeDtypeStruct(shape, kind) for (shape, kind), _ in outs],
        input_output_aliases=alias or {},
        compiler_params=pltpu.CompilerParams(vmem_limit_bytes=60 * 2**20),
        cost_estimate=pl.CostEstimate(flops=int(us * 0.3e9), bytes_accessed=0, transcendentals=0),
        name=name,
    )(*prefetch, *[array for array, _ in ins], *deps)


def whole(shape):
    return pl.BlockSpec(shape, lambda i, *s: (0,) * len(shape))


def load_pieces(dp_index, piece_refs, full_ref, sem, column=0):
    rows = piece_refs[0].shape[0]
    copies = []
    for r, piece in enumerate(piece_refs):
        spot = pl.multiple_of((dp_index ^ r) * rows, rows)
        if piece.shape[1] > full_ref.shape[1]:
            piece = piece.at[:, pl.ds(column, full_ref.shape[1])]
        copies.append(pltpu.make_async_copy(piece, full_ref.at[pl.ds(spot, rows)], sem.at[r]))
    for copy in copies:
        copy.start()
    return copies


def rope_tables():
    lane = jnp.arange(128, dtype=jnp.int32) % HS
    pair = (lane // 2).astype(f32)
    frequency = 10000.0 ** (-2.0 * pair / ROT)
    angles = jnp.arange(LEN, dtype=f32)[:, None] * frequency[None, :]
    turned = (lane < ROT)[None, :]
    cosine = jnp.where(turned, jnp.cos(angles), 1.0)
    sine = jnp.sin(angles)
    to_even = jnp.where(turned & (lane % 2 == 0)[None, :], -sine, 0.0)
    to_odd = jnp.where(turned & (lane % 2 == 1)[None, :], sine, 0.0)
    return cosine, to_even, to_odd


def turn(value, cosine, to_even, to_odd):
    return value * cosine + pltpu.roll(value, 127, 1) * to_even + pltpu.roll(value, 1, 1) * to_odd


def attend_kernel(pieces, info_ref, x_ref, back_ref, c_ref, e_ref, o_ref, *rest):
    piece_refs, rest = rest[:pieces], rest[pieces:]
    ctx_ref, grad_ref, out_ref, w_ref, joint_ref, dk_ref, dv_ref, sem = rest
    part = grad_ref.shape[1] // 3
    pair = pl.program_id(0)
    length, reverse = info_ref[0], info_ref[1]
    lane = lax.broadcasted_iota(jnp.int32, (1, 128), 1)
    zero = jnp.zeros((), bf16)

    @pl.when(pair == 0)
    def _():
        for copy in load_pieces(info_ref[2], piece_refs, w_ref, sem):
            copy.wait()

        def step(i, _):
            rows = pl.ds(pl.multiple_of(i * STRIP, STRIP), STRIP)
            values = mm(x_ref[rows, :], w_ref[...])
            for at in range(0, 3 * part, 128):
                piece = values[:, at : at + 128]
                if at < 2 * part:
                    piece = turn(piece, c_ref[rows, :], e_ref[rows, :], o_ref[rows, :])
                joint_ref[rows, at : at + 128] = piece.astype(bf16)
            return 0

        lax.fori_loop(0, LEN // STRIP, step, 0)

    q_at, k_at, v_at = (pl.ds(pl.multiple_of(g * part + pair * 128, 128), 128) for g in range(3))
    keys, values = joint_ref[:, k_at], joint_ref[:, v_at]
    back_all = back_ref[...].reshape(LEN, 128)
    key_heads, value_heads = [], []
    for head in range(2):
        inside = (lane // HS) == head
        key_heads.append(jnp.where(inside, keys, zero))
        value_heads.append(jnp.where(inside, values, zero))
    dk_ref[...] = jnp.zeros_like(dk_ref)
    dv_ref[...] = jnp.zeros_like(dv_ref)
    low = jnp.where(reverse == 0, 0, LEN - length)
    high = jnp.where(reverse == 0, length, LEN)
    q_id = lax.broadcasted_iota(jnp.int32, (BLOCK, BLOCK), 0)
    k_id = lax.broadcasted_iota(jnp.int32, (BLOCK, BLOCK), 1)

    def key_bias(start, size):
        spot = start + lax.broadcasted_iota(jnp.int32, (1, size), 1)
        return jnp.where((spot >= low) & (spot < high), 0.0, -1e30)

    def before(block, head):
        begin = block * BLOCK
        stop = begin + BLOCK
        rows = pl.ds(begin, BLOCK)
        inside = (lane // HS) == head
        query = joint_ref[rows, q_at] * jnp.asarray(1.0 / math.sqrt(HS), bf16)
        back = back_all[begin:stop]
        scores = mm(jnp.where(inside, query, zero), keys[:stop], NT)
        at_diag = jnp.where(k_id < q_id, key_bias(begin, BLOCK), jnp.where(k_id == q_id, 0.0, -1e30))
        tail = scores[:, begin:] + at_diag
        scores = jnp.concatenate([scores[:, :begin] + key_bias(0, begin), tail], axis=1) if begin else tail
        back_attend = mm(jnp.where(inside, back, zero), values[:stop], NT)
        return query, back, scores, back_attend

    def between(scores, back_attend):
        top = jnp.max(scores, axis=1, keepdims=True)
        exponent = jnp.exp(scores - top)
        attend = exponent * (1.0 / jnp.sum(exponent, axis=1, keepdims=True))
        delta = jnp.sum(attend * back_attend, axis=1, keepdims=True)
        return attend.astype(bf16), (attend * (back_attend - delta)).astype(bf16)

    kept = {}

    def behind(block, head, query, back, attend_low, grad_scores):
        begin = block * BLOCK
        stop = begin + BLOCK
        rows = pl.ds(begin, BLOCK)
        context = mm(attend_low, value_heads[head][:stop])
        grad_query = mm(grad_scores, key_heads[head][:stop])
        here = slice(head * HS, (head + 1) * HS)
        dk_ref[here, :stop] += mm(query.T[here], grad_scores)
        dv_ref[here, :stop] += mm(back.T[here], attend_low)
        if head == 0:
            kept[block] = context, grad_query
            return
        ctx_ref[rows, :] = (kept[block][0] + context).astype(bf16)
        grad_query = (kept[block][1] + grad_query) * (1.0 / math.sqrt(HS))
        grad_query = turn(grad_query, c_ref[rows, :], -e_ref[rows, :], -o_ref[rows, :])
        grad_ref[rows, q_at] = grad_query.astype(bf16)

    units = [(block, head) for block in range(LEN // BLOCK) for head in range(2)]
    coming, done = before(*units[0]), None
    for number, unit in enumerate(units):
        query, back, scores, back_attend = coming
        if number + 1 < len(units):
            coming = before(*units[number + 1])
        lows = between(scores, back_attend)
        if done is not None:
            behind(*done)
        done = (*unit, query, back, *lows)
    behind(*done)
    grad_key = turn(dk_ref[...].T, c_ref[...], -e_ref[...], -o_ref[...])
    grad_ref[:, k_at] = grad_key.astype(bf16)
    grad_ref[:, v_at] = dv_ref[...].T.astype(bf16)

    @pl.when(pair == pl.num_programs(0) - 1)
    def _():
        def step(i, _):
            rows = pl.ds(pl.multiple_of(i * STRIP, STRIP), STRIP)
            out_ref[rows, :] = mm(grad_ref[rows, :], w_ref[...], NT).astype(out_ref.dtype)
            return 0

        lax.fori_loop(0, LEN // STRIP, step, 0)


def attend(info, rows, pieces, back_rows, which, tables, kind):
    width, part = rows.shape[1], back_rows.shape[3]
    cols = 3 * part
    column = pl.BlockSpec((LEN, 128), lambda i, s: (0, i))
    blocks, _, local, _ = back_rows.shape
    back_spec = pl.BlockSpec((blocks, 1, local, 128), lambda i, s: (0, which, 0, i))
    ins = [(rows, whole((LEN, width))), (back_rows, back_spec)]
    ins += [(table, whole((LEN, 128))) for table in tables] + [(piece, anywhere) for piece in pieces]
    outs = [(((LEN, part), bf16), column), (((LEN, cols), bf16), whole((LEN, cols)))]
    outs.append((((LEN, width), kind), whole((LEN, width))))
    scratch = [
        pltpu.VMEM((width, cols), bf16),
        pltpu.VMEM((LEN, cols), bf16),
        pltpu.VMEM((128, LEN), f32),
        pltpu.VMEM((128, LEN), f32),
        pltpu.SemaphoreType.DMA((len(pieces),)),
    ]
    kernel = functools.partial(attend_kernel, len(pieces))
    return call(kernel, "attend", (part // 128,), [info], ins, outs, 40, scratch)


def norm_kernel(info_ref, x_ref, vec_ref, out_ref, own_ref):
    values = x_ref[0].astype(f32)
    centred = values - jnp.mean(values, -1, keepdims=True)
    spread = jnp.mean(centred * centred, -1, keepdims=True)
    normed = centred * lax.rsqrt(spread + norm_eps) * vec_ref[0:1, :] + vec_ref[1:2, :]
    low = normed.astype(bf16)
    out_ref[0] = low

    @pl.when(lax.rem(pl.program_id(0), 2) == info_ref[0])
    def _():
        own_ref[0] = low


def norm(info, tokens, vectors, deps=()):
    seqs, local, width = tokens.shape
    each = pl.BlockSpec((1, local, width), lambda i, s: (i, 0, 0))
    half = pl.BlockSpec((1, local, width), lambda i, s: (i // 2, 0, 0))
    ins = [(tokens, each), (vectors, whole(vectors.shape))]
    outs = [((tokens.shape, bf16), each), (((seqs // 2, local, width), bf16), half)]
    return call(norm_kernel, "norm", (seqs,), [info], ins, outs, 100, deps=deps)


def norm_back_kernel(order_ref, x_ref, cot_ref, vec_ref, bias_a_ref, bias_b_ref, back_ref, *rest):
    out_ref, sums_ref = rest[-2:]
    values = x_ref[0].astype(f32)
    centred = values - jnp.mean(values, -1, keepdims=True)
    spread = jnp.mean(centred * centred, -1, keepdims=True)
    scale = lax.rsqrt(spread + norm_eps)
    xhat = centred * scale
    back = back_ref[0].astype(f32)
    scaled = back * vec_ref[0:1, :]
    shift = jnp.mean(scaled, -1, keepdims=True)
    slope = jnp.mean(scaled * xhat, -1, keepdims=True)
    cot = cot_ref[0].astype(f32)
    out_ref[0] = cot + (scaled - shift - xhat * slope) * scale

    @pl.when(pl.program_id(0) == 0)
    def _():
        sums_ref[...] = jnp.zeros_like(sums_ref)
        width, half = x_ref.shape[2], bias_a_ref.shape[1]
        sums_ref[3:4, 0:half] = bias_a_ref[...]
        row, lane = 3 + half // width, half % width
        sums_ref[row : row + 1, lane : lane + half] = bias_b_ref[...]

    sums_ref[0:1, :] += jnp.sum(back * xhat, 0, keepdims=True)
    sums_ref[1:2, :] += jnp.sum(back, 0, keepdims=True)
    sums_ref[2:3, :] += jnp.sum(cot, 0, keepdims=True)


def norm_back(order, tokens, cotangent, back_normed, vectors, bias_sums, deps=(), earlier=None):
    seqs, local, width = tokens.shape
    count = back_normed.shape[0]
    picked = pl.BlockSpec((1, local, width), lambda i, s: (s[i], 0, 0))
    here = pl.BlockSpec((1, local, width), lambda i, s: (i, 0, 0))
    ins = [(tokens, picked), (cotangent, picked), (vectors, whole(vectors.shape))]
    ins += [(one, whole(one.shape)) for one in bias_sums] + [(back_normed, here)]
    alias = {}
    if earlier is not None:
        alias = {1 + len(ins): 0}
        ins.append((earlier, anywhere))
    outs = [((tokens.shape, f32), picked), (((8, width), f32), whole((8, width)))]
    return call(norm_back_kernel, "norm_back", (count,), [order], ins, outs, 7, deps=deps, alias=alias)


def back_context_kernel(pieces, column, info_ref, cot_ref, *rest):
    piece_refs, (out_ref, w_ref, sem) = rest[:pieces], rest[pieces:]
    local = out_ref.shape[2]

    @pl.when(pl.program_id(0) == 0)
    def _():
        for copy in load_pieces(info_ref[1], piece_refs, w_ref, sem, column):
            copy.wait()

    values = mm(cot_ref[...].reshape(2 * local, -1), w_ref[...]).astype(bf16)
    ahead = info_ref[4] == 0
    out_ref[0, 0] = jnp.where(ahead, values[:local], values[local:])
    out_ref[0, 1] = jnp.where(ahead, values[local:], values[:local])


def back_context_rows(info, cotangent, weights, column):
    seqs, local, width = cotangent.shape
    part = weights[0].shape[1] - column
    ins = [(cotangent, pl.BlockSpec((2, local, width), lambda i, s: (i, 0, 0)))]
    ins += [(piece, anywhere) for piece in weights]
    outs = [(((seqs // 2, 2, local, part), bf16), pl.BlockSpec((1, 2, local, part), lambda i, s: (i, 0, 0, 0)))]
    scratch = [pltpu.VMEM((width, part), bf16), pltpu.SemaphoreType.DMA((len(weights),))]
    kernel = functools.partial(back_context_kernel, len(weights), column)
    return call(kernel, "back_context", (seqs // 2,), [info], ins, outs, 6, scratch)


def feed_kernel(pieces, earlier, info_ref, x_ref, cot_ref, bias_ref, *rest):
    before, rest = rest[:earlier], rest[earlier:]
    piece_refs, rest = rest[:pieces], rest[pieces:]
    branch_ref, own_ref, away_ref, sums_ref, mine_ref, theirs_ref = rest[:6]
    w_ref, up_grad, down_grad, stage_ref, sem, out_sem = rest[6:]
    step = pl.program_id(0)
    width, hidden = up_grad.shape
    dp_index = info_ref[1]

    @pl.when(step == 0)
    def _():
        copies = load_pieces(dp_index, piece_refs, w_ref, sem)
        up_grad[...] = jnp.zeros_like(up_grad)
        down_grad[...] = jnp.zeros_like(down_grad)
        sums_ref[...] = jnp.zeros_like(sums_ref)
        for copy in copies:
            copy.wait()

    x = x_ref[...].reshape(-1, width)
    cot = cot_ref[...].reshape(-1, width)
    x_turned, cot_turned = x.T, cot.T
    rate = math.sqrt(2.0 / math.pi)
    back = jnp.zeros(x.shape, f32)
    branch = jnp.zeros(x.shape, f32)
    chunk = min(CHUNK, hidden)
    for at in range(0, hidden, chunk):
        cols = slice(at, at + chunk)
        up, down = w_ref[:, cols], w_ref[:, hidden + at : hidden + at + chunk]
        pre = mm(x, up) + bias_ref[:, cols]
        back_active = mm(cot, down)
        square = pre * pre
        bent = jnp.tanh(rate * pre * (1.0 + 0.044715 * square))
        half = 0.5 * (1.0 + bent)
        active = (pre * half).astype(bf16)
        slope = half + 0.5 * pre * (1.0 - bent * bent) * (rate * (1.0 + 3 * 0.044715 * square))
        grad_pre = (back_active * slope).astype(bf16)
        sums_ref[:, cols] += jnp.sum(grad_pre.astype(f32), 0, keepdims=True)
        branch += mm(active, down, NT)
        back += mm(grad_pre, up, NT)
        up_grad[:, cols] += mm(x_turned, grad_pre)
        down_grad[:, cols] += mm(cot_turned, active)
    if earlier:
        branch += before[0][...]
    branch_ref[...] = branch
    local = own_ref.shape[1]
    even = info_ref[0] == 0
    own = jnp.where(even, back[:local], back[local:])
    away = jnp.where(even, back[local:], back[:local])
    if earlier:
        own += before[1][0]
        away += before[2][0]
    own_ref[0] = own.astype(own_ref.dtype)
    away_ref[0] = away.astype(away_ref.dtype)

    @pl.when(step == pl.num_programs(0) - 1)
    def _():
        blocks = owner_blocks()
        rows = width // (2 * len(blocks))
        copies = []
        for number, (dp_half, seq) in enumerate(blocks):
            to = pl.ds(number * rows, rows)
            spot = owner_rows(info_ref, dp_half, seq, 1, rows)
            stage_ref[to, :hidden] = up_grad[spot, :].astype(bf16)
            stage_ref[to, hidden:] = down_grad[spot, :].astype(bf16)
            spot = owner_rows(info_ref, dp_half, seq, 0, rows)
            for side, source in enumerate((up_grad, down_grad)):
                target = mine_ref.at[to, pl.ds(side * hidden, hidden)]
                copies.append(pltpu.make_async_copy(source.at[spot], target, out_sem.at[2 * number + side]))
        copies.append(pltpu.make_async_copy(stage_ref, theirs_ref, out_sem.at[2 * len(blocks)]))
        for copy in copies:
            copy.start()
        for copy in copies:
            copy.wait()


def feed(info, normed, cotangent, bias, weights, before=(), deps=()):
    seqs, local, width = normed.shape
    rows, hidden = weights[0].shape[0], weights[0].shape[1] // 2
    pieces = len(weights)
    pair = pl.BlockSpec((2, local, width), lambda i, s: (i, 0, 0))
    half = pl.BlockSpec((1, local, width), lambda i, s: (i, 0, 0))
    flat = pl.BlockSpec((2 * local, width), lambda i, s: (i, 0))
    term_rows = pieces // 2 * rows
    kind = bf16 if before else f32
    ins = [(normed, pair), (cotangent, pair), (bias, whole((1, hidden)))]
    ins += list(zip(before, [flat, half, half])) + [(piece, anywhere) for piece in weights]
    outs = [
        (((seqs * local, width), f32), flat),
        (((seqs // 2, local, width), kind), half),
        (((seqs // 2, local, width), kind), half),
        (((1, hidden), f32), whole((1, hidden))),
        (((term_rows, 2 * hidden), f32), anywhere),
        (((term_rows, 2 * hidden), bf16), anywhere),
    ]
    scratch = [
        pltpu.VMEM((width, 2 * hidden), bf16),
        pltpu.VMEM((width, hidden), f32),
        pltpu.VMEM((width, hidden), f32),
        pltpu.VMEM((term_rows, 2 * hidden), bf16),
        pltpu.SemaphoreType.DMA((pieces,)),
        pltpu.SemaphoreType.DMA((2 * len(owner_blocks()) + 1,)),
    ]
    kernel = functools.partial(feed_kernel, pieces, len(before))
    return call(kernel, "feed", (seqs // 2,), [info], ins, outs, 37, scratch, deps)


def split_term(info_ref, sum_ref, mine_ref, theirs_ref):
    blocks = owner_blocks()
    rows = sum_ref.shape[0] // (2 * len(blocks))
    for number, (dp_half, seq) in enumerate(blocks):
        to = slice(number * rows, (number + 1) * rows)
        mine_ref[to, :] = sum_ref[owner_rows(info_ref, dp_half, seq, 0, rows), :]
        theirs_ref[to, :] = sum_ref[owner_rows(info_ref, dp_half, seq, 1, rows), :].astype(bf16)


def branch_kernel(last, pieces, column, order_ref, info_ref, context_ref, feed_ref, cot_ref, *rest):
    piece_refs, rest = rest[:pieces], rest[pieces:]
    before_ref = rest[0]
    own_ref, away_ref, rest = rest[last], rest[last + 1], rest[last + 2 :]
    w_ref, sem = rest[-2:]
    sum_ref = rest[-3]
    step = pl.program_id(0)

    @pl.when(step == 0)
    def _():
        for copy in load_pieces(info_ref[1], piece_refs, w_ref, sem, column):
            copy.wait()

    context = context_ref[0]
    share = own_ref.shape[2]
    own = pl.ds(pl.multiple_of(info_ref[2] * share, share), share)
    away = pl.ds(pl.multiple_of((1 - info_ref[2]) * share, share), share)
    own_ref[0] = feed_ref[0, :, own] + mm(context, w_ref[own, :], NT)
    away_ref[0] = (feed_ref[0, :, away] + mm(context, w_ref[away, :], NT)).astype(bf16)
    term = mm(cot_ref[0], context, TN)

    @pl.when(step == 0)
    def _():
        sum_ref[...] = term + before_ref[...] if last else term

    @pl.when(step > 0)
    def _():
        sum_ref[...] += term

    if last:

        @pl.when(step == pl.num_programs(0) - 1)
        def _():
            split_term(info_ref, sum_ref, *rest[:2])


def branch_rows(order, info, context, feed_branch, cotangent, weights, column, deps, before=None):
    count, local, part = context.shape
    width = cotangent.shape[2]
    last = before is not None
    half = pl.BlockSpec((1, local, width // 2), lambda i, s, t: (i, 0, 0))
    picked = pl.BlockSpec((1, local, width), lambda i, s, t: (s[i], 0, 0))
    ins = [(context, pl.BlockSpec((1, local, part), lambda i, s, t: (i, 0, 0)))]
    ins += [(feed_branch, picked), (cotangent, picked)] + [(piece, anywhere) for piece in weights]
    if last:
        ins.append((before, whole(before.shape)))
    terms = [((width // 2, part), f32), ((width // 2, part), bf16)] if last else [((width, part), f32)]
    outs = [(((count, local, width // 2), kind), half) for kind in (f32, bf16)]
    outs += [(term, whole(term[0])) for term in terms]
    scratch = [pltpu.VMEM((width, part), f32)] * last
    scratch += [pltpu.VMEM((width, part), bf16), pltpu.SemaphoreType.DMA((len(weights),))]
    kernel = functools.partial(branch_kernel, int(last), len(weights), column)
    return call(kernel, "branch", (count,), [order, info], ins, outs, 9, scratch, deps)


def output_kernel(info_ref, x_ref, own_ref, own_got_ref, other_ref, other_got_ref, vec_ref, out_ref):
    even = info_ref[0] == 0
    own = own_ref[0] + own_got_ref[0].astype(f32)
    other = other_ref[0] + other_got_ref[0].astype(f32)
    total = jnp.concatenate([jnp.where(even, own, other), jnp.where(even, other, own)], axis=0)
    out_ref[...] = (x_ref[...].astype(f32) + total + vec_ref[2:3, :]).astype(bf16)


def output_rows(info, tokens, own, own_got, other, other_got, params_here, deps):
    seqs, local, width = tokens.shape
    share = own.shape[2]
    half = pl.BlockSpec((1, local, share), lambda i, s: (i, 0, 0))
    ins = [(tokens.reshape(-1, width), pl.BlockSpec((2 * local, share), lambda i, s: (i, s[2])))]
    ins += [(one, half) for one in (own, own_got, other, other_got)] + [(params_here, whole(params_here.shape))]
    outs = [(((seqs * local, share), bf16), pl.BlockSpec((2 * local, share), lambda i, s: (i, 0)))]
    return call(output_kernel, "output", (seqs // 2,), [info], ins, outs, 6, deps=deps)[0]


def joint_term_kernel(count, info_ref, *refs):
    xs, grads, (mine_ref, theirs_ref, sum_ref) = refs[:count], refs[count : 2 * count], refs[2 * count :]
    term = mm(xs[0][...], grads[0][...], TN)
    for x, grad in zip(xs[1:], grads[1:]):
        term += mm(x[...], grad[...], TN)
    sum_ref[...] = term
    steps = pl.num_programs(0) // 2
    order = seq_order()
    rows = term.shape[0] // len(order)
    parts = [sum_ref[pl.ds(pl.multiple_of((info_ref[3] ^ seq) * rows, rows), rows), :] for seq in order]

    @pl.when(pl.program_id(0) < steps)
    def _():
        for number, part in enumerate(parts):
            theirs_ref[number * rows : (number + 1) * rows, :] = part.astype(bf16)

    @pl.when(pl.program_id(0) >= steps)
    def _():
        for number, part in enumerate(parts):
            mine_ref[number * rows : (number + 1) * rows, :] = part


def joint_term(info, xs, grads, deps):
    pieces = lax.axis_size("dp")
    steps = pieces // 2
    width, cols = xs[0].shape[1], grads[0].shape[1]
    rows = width // pieces

    def picked(i, s):
        return (0, s[1] ^ (2 * lax.rem(i, steps) + 1 - i // steps))

    ins = [(x, pl.BlockSpec((LEN, rows), picked)) for x in xs] + [(grad, whole((LEN, cols))) for grad in grads]
    outs = [
        (((steps * rows, cols), f32), pl.BlockSpec((rows, cols), lambda i, s: (jnp.maximum(i - steps, 0), 0))),
        (((steps * rows, cols), bf16), pl.BlockSpec((rows, cols), lambda i, s: (jnp.minimum(i, steps - 1), 0))),
    ]
    scratch = [pltpu.VMEM((rows, cols), f32)]
    kernel = functools.partial(joint_term_kernel, len(xs))
    return call(kernel, "joint_term", (pieces,), [info], ins, outs, 12, scratch, deps)


def halves(values):
    high = values.astype(bf16)
    return high, (values - high.astype(f32)).astype(bf16)


def mm3(a, b, dims):
    a_high, a_low = a
    b_high, b_low = b
    return mm(a_high, b_high, dims) + (mm(a_high, b_low, dims) + mm(a_low, b_high, dims))


def shampoo_kernel(fan, flipped, g_ref, w_ref, big_ref, small_ref, root_ref, small_root_ref, *rest):
    big_out, small_out, w_out, left_ref, right_ref, sg_ref, turned_ref = rest
    step = pl.program_id(0)
    rows, block = g_ref.shape[0], big_ref.shape[0]
    cols = pl.ds(pl.multiple_of(step * block, block), block)

    @pl.when(step == 0)
    def _():
        g = halves(g_ref[...])
        left_ref[...] = jnp.concatenate([g[0], g[1], g[0]], axis=0)
        right_ref[...] = jnp.concatenate([g[0], g[0], g[1]], axis=0)
        turned = mm3(halves(small_root_ref[...]), g, TN if flipped else NN)
        sg_ref[...] = jnp.concatenate(halves(turned), axis=0)
        small_out[...] = beta_stats * small_ref[...] + (1.0 - beta_stats) * mm3(g, g, NT)

    big_out[...] = beta_stats * big_ref[...] + (1.0 - beta_stats) * mm(left_ref[:, cols], right_ref[...], TN)
    root_high, root_low = halves(root_ref[...])
    if flipped:
        both = mm(sg_ref[...], root_high, NT)
        turned_ref[:, cols] = both[:rows] + both[rows:] + mm(sg_ref[:rows, :], root_low, NT)
    else:
        both = mm(sg_ref[:, cols], root_high)
        part = both[:rows] + both[rows:] + mm(sg_ref[:rows, cols], root_low)

        @pl.when(step == 0)
        def _():
            turned_ref[...] = part

        @pl.when(step > 0)
        def _():
            turned_ref[...] += part

    @pl.when(step == pl.num_programs(0) - 1)
    def _():
        turned = turned_ref[...]
        square = jnp.sum(turned * turned, axis=(0, 1), keepdims=True) * (1.0 / turned.size)
        w_out[...] = w_ref[...] - rate_matrix / math.sqrt(fan) * turned * lax.rsqrt(square + 1e-06)


def shampoo(gradient, weight, big, small, big_root, small_root, fan, flipped, deps=()):
    rows, size = gradient.shape
    block = min(STRIP, size)
    if size % block:
        block = size
    strip = pl.BlockSpec((block, size), lambda i: (i, 0))
    square = whole((rows, rows))
    flat = whole((rows, size))
    ins = [(gradient, flat), (weight, flat), (big, strip), (small, square), (big_root, strip), (small_root, square)]
    outs = [(((size, size), f32), strip), (((rows, rows), f32), square), (((rows, size), f32), flat)]
    scratch = [
        pltpu.VMEM((3 * rows, size), bf16),
        pltpu.VMEM((3 * rows, size), bf16),
        pltpu.VMEM((2 * rows, size), bf16),
        pltpu.VMEM((rows, size), f32),
    ]
    kernel = functools.partial(shampoo_kernel, fan, flipped)
    return call(kernel, "shampoo", (size // block,), [], ins, outs, 19 * size * size / 2048**2, scratch, deps)


def diagonal_rule(values, moment, gradient):
    moment_new = beta_moment * moment + (1.0 - beta_moment) * gradient * gradient
    return (moment_new, values - rate_vector * gradient / (jnp.sqrt(moment_new) + 1e-08))


def body(
    tokens,
    cotangent,
    lengths,
    orientation,
    joint_weight,
    output_weight,
    expand_weight,
    shrink_weight,
    norm_params,
    expand_bias,
    norm_moment,
    bias_moment,
    joint_left,
    joint_right,
    joint_left_root,
    joint_right_root,
    output_left,
    output_right,
    output_left_root,
    output_right_root,
    expand_left,
    expand_right,
    expand_left_root,
    expand_right_root,
    shrink_left,
    shrink_right,
    shrink_left_root,
    shrink_right_root,
):
    n_mp, n_seq, n_dp = lax.axis_size("mp"), lax.axis_size("seq"), lax.axis_size("dp")
    mp_index, seq_index, dp_index = lax.axis_index("mp"), lax.axis_index("seq"), lax.axis_index("dp")
    seqs, local, width = tokens.shape
    rows = seqs * local
    share = norm_params.shape[1]
    per = seqs // n_seq
    paired = n_mp == 2 and per == 2
    flip = mp_index if paired else jnp.zeros((), jnp.int32)
    ids = [1 - flip, flip] if paired else list(range(per))
    info = jnp.stack([flip, dp_index, mp_index, seq_index, jnp.asarray(ids[0])]).astype(jnp.int32)

    def facts(which):
        spot = seq_index * per + which
        values = [lax.dynamic_index_in_dim(one, spot, 0, False) for one in (lengths, orientation)]
        return jnp.stack(values + [dp_index])

    def own_share(values):
        return lax.dynamic_slice_in_dim(values, mp_index * share, share, values.ndim - 1)

    def to_whole(values):
        return lax.all_to_all(values, "seq", 0, 0, tiled=True)

    output_t, shrink_t = output_weight.T, shrink_weight.T
    hidden = expand_weight.shape[1]
    half = hidden // 2
    both = lambda left, right: jnp.concatenate([left.astype(bf16), right.astype(bf16)], axis=1)
    early = Gather(both(expand_weight[:, :half], shrink_t[:, :half]))
    middle = Gather(both(joint_weight, output_t))
    late = Gather(both(expand_weight[:, half:], shrink_t[:, half:]))
    along = len(bits_of(n_seq))

    early.value, params_here = tie(early.value, norm_params)
    if paired:
        other_params = swap(params_here, "mp", 1)
        upper = mp_index != 0
        vectors = jnp.concatenate(
            [jnp.where(upper, other_params, norm_params), jnp.where(upper, norm_params, other_params)], axis=1
        )
    else:
        vectors = lax.all_gather(params_here, "mp", axis=1, tiled=True)
    tables = rope_tables()
    facts_of = [facts(which) for which in ids]
    normed, normed_own = norm(info, tokens, vectors)
    early.step()
    early.value, middle.value, late.value, normed, normed_own = tie(
        early.value, middle.value, late.value, normed, normed_own
    )
    for _ in range(1, along):
        early.step()
    middle.step()
    early.value, middle.value, late.value = tie(early.value, middle.value, late.value)
    for _ in range(1, along):
        middle.step()
    late.step()
    while len(early.todo) > 1:
        early.step()
    (middle.value, late.value, normed_own), (early.pieces,) = beside(
        [middle.value, late.value, normed_own], early.pieces
    )
    early.step()
    while len(middle.todo) > 1:
        middle.step()
    for _ in range(1, along):
        late.step()
    (late.value, normed_own), (early.pieces, tables, facts_of) = beside(
        [late.value, normed_own], early.pieces, list(tables), facts_of
    )
    while len(late.todo) > 1:
        late.step()

    if paired:
        arrived = [to_whole(normed_own).reshape(LEN, width)]
    else:
        split = normed.reshape(n_seq, per, local, width)
        arrived = [to_whole(split[:, t]).reshape(LEN, width) for t in range(per)]

    first = feed(info, normed, cotangent, expand_bias[None, :half], early.pieces, deps=[late.pieces[0]])
    first, (middle.pieces,) = beside(first, middle.pieces)
    middle.step()
    scatter_early = Scatter(first[4], first[5])
    (scatter_early.away,), (middle.pieces, late.pieces, arrived) = beside(
        [scatter_early.away], middle.pieces, late.pieces, arrived
    )
    late.step()
    scatter_early.step()
    normed_seqs = [swap(arrived[0], "mp", 1), arrived[0]] if paired else arrived
    joint_cols = joint_weight.shape[1]
    part = joint_cols // 3
    back_parts = back_context_rows(info, cotangent, middle.pieces, joint_cols)
    back_parts, (late.pieces, scatter_early.terms[-1]) = beside(back_parts, late.pieces, scatter_early.terms[-1])
    back_whole = to_whole(back_parts[0])
    scatter_early.step()
    second = feed(info, normed, cotangent, expand_bias[None, half:], late.pieces, first[:3])
    second, (normed_seqs, back_whole, scatter_early.terms[-1]) = beside(
        second, normed_seqs, back_whole, scatter_early.terms[-1]
    )
    feed_branch, ffn_own, ffn_away = second[:3]
    known = [first[3], second[3]]

    fans = (width, width // 32, width, 4 * width)
    expand_state = (expand_weight, expand_right, expand_left, expand_right_root, expand_left_root, fans[2], False)
    shrink_state = (shrink_t, shrink_left, shrink_right, shrink_left_root, shrink_right_root, fans[3], True)
    joint_state = (joint_weight, joint_right, joint_left, joint_right_root, joint_left_root, fans[0], False)
    output_state = (output_t, output_left, output_right, output_left_root, output_right_root, fans[1], True)
    kind = bf16 if paired else f32
    scatter_late = Scatter(second[4], second[5])
    scatter_late.step()
    scatter_early.step()
    scatter_late.step()
    attended = attend(facts_of[0], normed_seqs[0], middle.pieces, back_whole, 0, tables, kind)
    attended, (scatter_early.terms[-1], scatter_late.terms[-1]) = beside(
        attended, scatter_early.terms[-1], scatter_late.terms[-1]
    )
    context_other, grad_other, back_other = attended
    received = [swap(back_other, "mp", 1)] if paired else []
    context_other = to_whole(context_other.reshape(n_seq, local, part))
    scatter_early.step()
    scatter_late.step()
    attended = attend(facts_of[1], normed_seqs[1], middle.pieces, back_whole, 1, tables, kind)
    attended, (ffn_away, received, context_other, scatter_early.terms[-1], scatter_late.terms[-1]) = beside(
        attended, ffn_away, received, context_other, scatter_early.terms[-1], scatter_late.terms[-1]
    )
    context_own, grad_own, back_own = attended
    context_own = context_own.reshape(n_seq, local, part)
    grads = [grad_other, grad_own]

    def feed_grads():
        early_grad, late_grad = scatter_early.finish(), scatter_late.finish()
        expand_grad = jnp.concatenate([early_grad[:, :half], late_grad[:, :half]], axis=1)
        return expand_grad, jnp.concatenate([early_grad[:, half:], late_grad[:, half:]], axis=1)

    if paired:
        order = jnp.arange(n_seq, dtype=jnp.int32) * 2
        own_order, other_order = order + flip, order + 1 - flip
        back_sum = (back_own.astype(f32) + received[0].astype(f32)).astype(bf16)
        scatter_late.step()
        ffn_got = swap(ffn_away, "mp", 1)
        context_own = to_whole(context_own)
        branch_in = feed_branch.reshape(tokens.shape)
        branched = branch_rows(
            other_order, info, context_other, branch_in, cotangent, middle.pieces, joint_cols, [back_sum]
        )
        other_own, other_away, output_term = branched
        own_got = swap(other_away, "mp", 1)
        joint_parts = joint_term(info, normed_seqs, grads, [output_term])
        joint_parts, (context_own, back_sum) = beside(joint_parts, context_own, back_sum)
        back_sum = to_whole(back_sum.reshape(n_seq, local, width))
        expand_grad, shrink_grad = feed_grads()
        scatter_joint = Scatter(*joint_parts)
        scatter_joint.step()
        expand_new = shampoo(expand_grad, *expand_state, [joint_parts[0]])
        expand_new, (scatter_joint.terms[-1], ffn_got) = beside(expand_new, scatter_joint.terms[-1], ffn_got)
        scatter_joint.step()
        branched = branch_rows(
            own_order, info, context_own, branch_in, cotangent, middle.pieces, joint_cols, [expand_new[1]], output_term
        )
        own_own, own_away, output_mine, output_theirs = branched
        other_got = swap(own_away, "mp", 1)
        scatter_output = Scatter(output_mine, output_theirs)
        scatter_output.step()
        shrink_new = shampoo(shrink_grad, *shrink_state, [output_mine])
        shrink_new, (back_sum, scatter_joint.terms[-1], scatter_output.terms[-1]) = beside(
            shrink_new, back_sum, scatter_joint.terms[-1], scatter_output.terms[-1]
        )
        scatter_joint.step()
        scatter_output.step()
        total = ffn_own.astype(f32) + ffn_got.astype(f32) + back_sum.astype(f32)
        total = total.astype(bf16)
        total_other = swap(total, "mp", 1)
        backed = norm_back(own_order, tokens, cotangent, total, vectors, known, [shrink_new[1]])
        backed, (scatter_joint.terms[-1], scatter_output.terms[-1], own_got, other_got) = beside(
            backed, scatter_joint.terms[-1], scatter_output.terms[-1], own_got, other_got
        )
        input_grad, sums = backed
        scatter_joint.step()
        scatter_output.step()
        hops = [(axis, bit) for axis in ("dp", "seq") for bit in bits_of(lax.axis_size(axis))]
        vector_terms = sums
        vector_got = swap(vector_terms, *hops[0])
        block_output = output_rows(
            info, tokens, own_own, own_got, other_own, other_got, norm_params, [sums]
        )
        (block_output,), (scatter_joint.terms[-1], scatter_output.terms[-1], vector_got) = beside(
            [block_output], scatter_joint.terms[-1], scatter_output.terms[-1], vector_got
        )
        block_output = block_output.reshape(seqs, local, share)
        vector_terms = vector_terms + vector_got
        vector_got = swap(vector_terms, *hops[1])
        joint_grad = scatter_joint.finish()
        scatter_output.step()
        joint_new = shampoo(joint_grad, *joint_state, [block_output])
        joint_new, (scatter_output.terms[-1], vector_got) = beside(
            joint_new, scatter_output.terms[-1], vector_got
        )
        vector_terms = vector_terms + vector_got
        vector_got = swap(vector_terms, *hops[2])
        output_grad = scatter_output.finish()
        output_new = shampoo(output_grad, *output_state, [joint_new[1]])
        output_new, (total_other, vector_got) = beside(output_new, total_other, vector_got)
        vector_terms = vector_terms + vector_got
        vector_got = swap(vector_terms, *hops[3])
        backed = norm_back(other_order, tokens, cotangent, total_other, vectors, known, [], input_grad)
        backed, (vector_got,) = beside(backed, vector_got)
        input_grad = backed[0]
        vector_terms = vector_terms + vector_got
        for hop in hops[4:]:
            vector_terms = vector_terms + swap(vector_terms, *hop)
        sums, bias_grad = vector_terms[:3], vector_terms[3:].reshape(-1)[:hidden]
        away_share = lax.dynamic_slice_in_dim(sums, (1 - mp_index) * share, share, 1)
        norm_grad = own_share(sums) + swap(away_share, "mp", 1)
    else:
        context_own = to_whole(context_own)
        context = jnp.stack([context_other, context_own], axis=1).reshape(rows, part)
        output_full = merge_pieces([piece[:, joint_cols:] for piece in middle.pieces])
        branch = feed_branch + mm(context, output_full, NT)
        summed = lax.psum_scatter(branch, "mp", scatter_dimension=1, tiled=True).reshape(seqs, local, share)
        block_output = (own_share(tokens).astype(f32) + summed + norm_params[2]).astype(bf16)
        output_term = mm(cotangent.reshape(rows, width), context, TN).reshape(n_dp, n_seq, -1, part)
        pick = lambda dp_half, seq, other: output_term[dp_index ^ (2 * dp_half + other), seq_index ^ seq]
        output_mine, output_theirs = (
            jnp.concatenate([pick(*block, other) for block in owner_blocks()]) for other in (0, 1)
        )
        back = [lax.psum(one, "mp") for one in (back_other, back_own)]
        back = [to_whole(one.astype(bf16).reshape(n_seq, local, width)) for one in back]
        feed_back = jnp.stack([ffn_own, ffn_away], axis=1).astype(f32)
        total = jnp.stack(back, axis=1).astype(f32) + lax.psum(feed_back, "mp")
        total = total.astype(bf16).reshape(seqs, local, width)
        input_grad, sums = norm_back(jnp.arange(seqs, dtype=jnp.int32), tokens, cotangent, total, vectors, known)
        joint_grad = Scatter(*joint_term(info, normed_seqs, grads, [])).finish()
        output_grad = Scatter(output_mine, output_theirs.astype(bf16)).finish()
        expand_grad, shrink_grad = feed_grads()
        expand_new = shampoo(expand_grad, *expand_state)
        shrink_new = shampoo(shrink_grad, *shrink_state)
        joint_new = shampoo(joint_grad, *joint_state)
        output_new = shampoo(output_grad, *output_state)
        vector_terms = sums
        for axis in ("dp", "seq"):
            for bit in bits_of(lax.axis_size(axis)):
                vector_terms = vector_terms + swap(vector_terms, axis, bit)
        norm_grad, bias_grad = own_share(vector_terms[:3]), vector_terms[3:].reshape(-1)[:hidden]

    joint_right_new, joint_left_new, joint_new = joint_new
    output_left_new, output_right_new, output_new = output_new
    expand_right_new, expand_left_new, expand_new = expand_new
    shrink_left_new, shrink_right_new, shrink_new = shrink_new
    norm_moment_new, norm_params_new = diagonal_rule(norm_params, norm_moment, norm_grad)
    bias_moment_new, bias_new = diagonal_rule(expand_bias, bias_moment, bias_grad)
    return (
        block_output,
        input_grad,
        joint_grad,
        output_grad.T,
        expand_grad,
        shrink_grad.T,
        norm_grad,
        bias_grad,
        joint_left_new,
        joint_right_new,
        output_left_new,
        output_right_new,
        expand_left_new,
        expand_right_new,
        shrink_left_new,
        shrink_right_new,
        joint_new,
        output_new.T,
        expand_new,
        shrink_new.T,
        norm_moment_new,
        bias_moment_new,
        norm_params_new,
        bias_new,
    )


def solution(mesh):
    data = P("dp", "seq", None)
    rows = P(("dp", "seq"), "mp")
    cols = P("mp", ("dp", "seq"))
    vector = P(None, "mp")
    placed = (data, data, P("dp"), P("dp"), rows, cols, rows, cols, vector, P("mp"), vector, P("mp")) + (rows,) * 16
    out_placed = (
        (P("dp", "seq", "mp"), data, rows, cols, rows, cols, vector, P("mp"))
        + (rows,) * 8
        + (rows, cols, rows, cols, vector, P("mp"), vector, P("mp"))
    )
    return jax.shard_map(body, mesh=mesh, in_specs=placed, out_specs=out_placed, check_vma=False)
```

```python
import functools
import math

import jax
import jax.numpy as jnp
from jax import lax
from jax.experimental import pallas as pl
from jax.experimental.pallas import tpu as pltpu
from jax.sharding import PartitionSpec as P

HS = 64
ROT = 32
LEN = 1024
BLOCK = 256
CHUNK = 1024
STRIP = 512

norm_eps = 1e-05
beta_stats = 0.95
beta_moment = 0.95
rate_matrix = 0.5
rate_vector = 0.03
bf16 = jnp.bfloat16
f32 = jnp.float32
NT = (((1,), (1,)), ((), ()))
TN = (((0,), (0,)), ((), ()))
NN = (((1,), (0,)), ((), ()))
anywhere = pl.BlockSpec(memory_space=pl.ANY)


def mm(a, b, dims=NN):
    return lax.dot_general(a, b, dims, preferred_element_type=f32)


def bits_of(size):
    return [1 << i for i in range(size.bit_length() - 1)]


def swap(value, axis, bit):
    size = lax.axis_size(axis)
    return lax.ppermute(value, axis, [(i, i ^ bit) for i in range(size)])


def tie(*values):
    return lax.optimization_barrier(values)


def beside(outs, *groups):
    flat = list(outs)
    for group in groups:
        flat += group if isinstance(group, list) else [group]
    flat = list(tie(*flat))
    outs, flat = flat[: len(outs)], flat[len(outs) :]
    result = []
    for group in groups:
        count = len(group) if isinstance(group, list) else 1
        result.append(flat[:count] if isinstance(group, list) else flat[0])
        flat = flat[count:]
    return outs, result


class Gather:
    def __init__(self, shard):
        self.shape = shard.shape
        self.value = shard
        self.todo = [("seq", bit) for bit in reversed(bits_of(lax.axis_size("seq")))]
        self.todo += [("dp", bit) for bit in reversed(bits_of(lax.axis_size("dp")))]
        self.pieces = None
        self.order = [0]

    def step(self):
        axis, bit = self.todo.pop(0)
        if axis == "seq":
            rows = self.shape[0]
            mine, other = self.value, swap(self.value, "seq", bit)
            upper = (lax.axis_index("seq") & bit) != 0
            parts = []
            for at in range(0, mine.shape[0], rows):
                one, two = mine[at : at + rows], other[at : at + rows]
                parts += [jnp.where(upper, two, one), jnp.where(upper, one, two)]
            self.value = jnp.concatenate(parts, axis=0)
            return
        if self.pieces is None:
            self.pieces = [self.value]
        self.pieces = self.pieces + [swap(piece, "dp", bit) for piece in self.pieces]
        self.order = self.order + [r ^ bit for r in self.order]
        if not self.todo:
            self.pieces = [piece for _, piece in sorted(zip(self.order, self.pieces), key=lambda item: item[0])]


def merge_pieces(pieces):
    index = lax.axis_index("dp")
    for bit in bits_of(len(pieces)):
        upper = (index & bit) != 0
        pieces = [jnp.where(upper, pieces[r ^ bit], pieces[r]) for r in range(len(pieces))]
    return jnp.concatenate(pieces, axis=0)


class Scatter:
    def __init__(self, mine, theirs):
        n_dp, n_seq = lax.axis_size("dp"), lax.axis_size("seq")
        self.cols = mine.shape[1]
        self.terms, self.away = [mine], theirs
        self.now = ("dp", 1)
        self.todo = [("dp", bit) for bit in reversed(bits_of(n_dp)[1:])]
        self.todo += [("seq", bit) for bit in bits_of(n_seq)]

    def step(self):
        if self.away is None:
            self.now = self.todo.pop(0)
            rows = self.terms[0].shape[0] // 2
            self.away = sum(term[rows:].astype(f32) for term in self.terms).astype(bf16)
            self.terms = [term[:rows] for term in self.terms]
        self.sent = self.away
        self.terms = self.terms + [swap(self.away, *self.now)]
        self.away = None

    def finish(self):
        while self.todo or self.away is not None:
            self.step()
        return sum(term.astype(f32) for term in self.terms)


def owner_rows(info_ref, dp_half, seq, other, rows):
    block = (info_ref[1] ^ (2 * dp_half + other)) * lax.axis_size("seq") + (info_ref[3] ^ seq)
    return pl.ds(pl.multiple_of(block * rows, rows), rows)


def seq_order():
    order = [0]
    for bit in reversed(bits_of(lax.axis_size("seq"))):
        order = order + [place | bit for place in order]
    return order


def owner_blocks():
    return [(dp_half, seq) for dp_half in range(lax.axis_size("dp") // 2) for seq in seq_order()]


def call(kernel, name, grid, prefetch, ins, outs, us, scratch=(), deps=(), alias=None):
    count = len(prefetch) + len(ins)

    def run(*refs):
        kernel(*refs[:count], *refs[count + len(deps) :])

    return pl.pallas_call(
        run,
        grid_spec=pltpu.PrefetchScalarGridSpec(
            num_scalar_prefetch=len(prefetch),
            grid=grid,
            in_specs=[spec for _, spec in ins] + [anywhere] * len(deps),
            out_specs=[spec for _, spec in outs],
            scratch_shapes=list(scratch),
        ),
        out_shape=[jax.ShapeDtypeStruct(shape, kind) for (shape, kind), _ in outs],
        input_output_aliases=alias or {},
        compiler_params=pltpu.CompilerParams(vmem_limit_bytes=60 * 2**20),
        cost_estimate=pl.CostEstimate(flops=int(us * 0.3e9), bytes_accessed=0, transcendentals=0),
        name=name,
    )(*prefetch, *[array for array, _ in ins], *deps)


def whole(shape):
    return pl.BlockSpec(shape, lambda i, *s: (0,) * len(shape))


def load_pieces(dp_index, piece_refs, full_ref, sem, column=0):
    rows = piece_refs[0].shape[0]
    copies = []
    for r, piece in enumerate(piece_refs):
        spot = pl.multiple_of((dp_index ^ r) * rows, rows)
        if piece.shape[1] > full_ref.shape[1]:
            piece = piece.at[:, pl.ds(column, full_ref.shape[1])]
        copies.append(pltpu.make_async_copy(piece, full_ref.at[pl.ds(spot, rows)], sem.at[r]))
    for copy in copies:
        copy.start()
    return copies


def rope_tables():
    lane = jnp.arange(128, dtype=jnp.int32) % HS
    pair = (lane // 2).astype(f32)
    frequency = 10000.0 ** (-2.0 * pair / ROT)
    angles = jnp.arange(LEN, dtype=f32)[:, None] * frequency[None, :]
    turned = (lane < ROT)[None, :]
    cosine = jnp.where(turned, jnp.cos(angles), 1.0)
    sine = jnp.sin(angles)
    to_even = jnp.where(turned & (lane % 2 == 0)[None, :], -sine, 0.0)
    to_odd = jnp.where(turned & (lane % 2 == 1)[None, :], sine, 0.0)
    return cosine, to_even, to_odd


def turn(value, cosine, to_even, to_odd):
    return value * cosine + pltpu.roll(value, 127, 1) * to_even + pltpu.roll(value, 1, 1) * to_odd


def attend_kernel(pieces, info_ref, x_ref, back_ref, c_ref, e_ref, o_ref, *rest):
    piece_refs, rest = rest[:pieces], rest[pieces:]
    ctx_ref, grad_ref, out_ref, w_ref, joint_ref, dk_ref, dv_ref, sem = rest
    part = grad_ref.shape[1] // 3
    pair = pl.program_id(0)
    length, reverse = info_ref[0], info_ref[1]
    lane = lax.broadcasted_iota(jnp.int32, (1, 128), 1)
    zero = jnp.zeros((), bf16)

    @pl.when(pair == 0)
    def _():
        for copy in load_pieces(info_ref[2], piece_refs, w_ref, sem):
            copy.wait()

        def step(i, _):
            rows = pl.ds(pl.multiple_of(i * STRIP, STRIP), STRIP)
            values = mm(x_ref[rows, :], w_ref[...])
            for at in range(0, 3 * part, 128):
                piece = values[:, at : at + 128]
                if at < 2 * part:
                    piece = turn(piece, c_ref[rows, :], e_ref[rows, :], o_ref[rows, :])
                joint_ref[rows, at : at + 128] = piece.astype(bf16)
            return 0

        lax.fori_loop(0, LEN // STRIP, step, 0)

    q_at, k_at, v_at = (pl.ds(pl.multiple_of(g * part + pair * 128, 128), 128) for g in range(3))
    keys, values = joint_ref[:, k_at], joint_ref[:, v_at]
    back_all = back_ref[...].reshape(LEN, 128)
    key_heads, value_heads = [], []
    for head in range(2):
        inside = (lane // HS) == head
        key_heads.append(jnp.where(inside, keys, zero))
        value_heads.append(jnp.where(inside, values, zero))
    dk_ref[...] = jnp.zeros_like(dk_ref)
    dv_ref[...] = jnp.zeros_like(dv_ref)
    low = jnp.where(reverse == 0, 0, LEN - length)
    high = jnp.where(reverse == 0, length, LEN)
    q_id = lax.broadcasted_iota(jnp.int32, (BLOCK, BLOCK), 0)
    k_id = lax.broadcasted_iota(jnp.int32, (BLOCK, BLOCK), 1)

    def key_bias(start, size):
        spot = start + lax.broadcasted_iota(jnp.int32, (1, size), 1)
        return jnp.where((spot >= low) & (spot < high), 0.0, -1e30)

    def before(block, head):
        begin = block * BLOCK
        stop = begin + BLOCK
        rows = pl.ds(begin, BLOCK)
        inside = (lane // HS) == head
        query = joint_ref[rows, q_at] * jnp.asarray(1.0 / math.sqrt(HS), bf16)
        back = back_all[begin:stop]
        scores = mm(jnp.where(inside, query, zero), keys[:stop], NT)
        at_diag = jnp.where(k_id < q_id, key_bias(begin, BLOCK), jnp.where(k_id == q_id, 0.0, -1e30))
        tail = scores[:, begin:] + at_diag
        scores = jnp.concatenate([scores[:, :begin] + key_bias(0, begin), tail], axis=1) if begin else tail
        back_attend = mm(jnp.where(inside, back, zero), values[:stop], NT)
        return query, back, scores, back_attend

    def between(scores, back_attend):
        top = jnp.max(scores, axis=1, keepdims=True)
        exponent = jnp.exp(scores - top)
        attend = exponent * (1.0 / jnp.sum(exponent, axis=1, keepdims=True))
        delta = jnp.sum(attend * back_attend, axis=1, keepdims=True)
        return attend.astype(bf16), (attend * (back_attend - delta)).astype(bf16)

    kept = {}

    def behind(block, head, query, back, attend_low, grad_scores):
        begin = block * BLOCK
        stop = begin + BLOCK
        rows = pl.ds(begin, BLOCK)
        context = mm(attend_low, value_heads[head][:stop])
        grad_query = mm(grad_scores, key_heads[head][:stop])
        here = slice(head * HS, (head + 1) * HS)
        dk_ref[here, :stop] += mm(query.T[here], grad_scores)
        dv_ref[here, :stop] += mm(back.T[here], attend_low)
        if head == 0:
            kept[block] = context, grad_query
            return
        ctx_ref[rows, :] = (kept[block][0] + context).astype(bf16)
        grad_query = (kept[block][1] + grad_query) * (1.0 / math.sqrt(HS))
        grad_query = turn(grad_query, c_ref[rows, :], -e_ref[rows, :], -o_ref[rows, :])
        grad_ref[rows, q_at] = grad_query.astype(bf16)

    units = [(block, head) for block in range(LEN // BLOCK) for head in range(2)]
    coming, done = before(*units[0]), None
    for number, unit in enumerate(units):
        query, back, scores, back_attend = coming
        if number + 1 < len(units):
            coming = before(*units[number + 1])
        lows = between(scores, back_attend)
        if done is not None:
            behind(*done)
        done = (*unit, query, back, *lows)
    behind(*done)
    grad_key = turn(dk_ref[...].T, c_ref[...], -e_ref[...], -o_ref[...])
    grad_ref[:, k_at] = grad_key.astype(bf16)
    grad_ref[:, v_at] = dv_ref[...].T.astype(bf16)

    @pl.when(pair == pl.num_programs(0) - 1)
    def _():
        def step(i, _):
            rows = pl.ds(pl.multiple_of(i * STRIP, STRIP), STRIP)
            out_ref[rows, :] = mm(grad_ref[rows, :], w_ref[...], NT).astype(out_ref.dtype)
            return 0

        lax.fori_loop(0, LEN // STRIP, step, 0)


def attend(info, rows, pieces, back_rows, which, tables, kind):
    width, part = rows.shape[1], back_rows.shape[3]
    cols = 3 * part
    column = pl.BlockSpec((LEN, 128), lambda i, s: (0, i))
    blocks, _, local, _ = back_rows.shape
    back_spec = pl.BlockSpec((blocks, 1, local, 128), lambda i, s: (0, which, 0, i))
    ins = [(rows, whole((LEN, width))), (back_rows, back_spec)]
    ins += [(table, whole((LEN, 128))) for table in tables] + [(piece, anywhere) for piece in pieces]
    outs = [(((LEN, part), bf16), column), (((LEN, cols), bf16), whole((LEN, cols)))]
    outs.append((((LEN, width), kind), whole((LEN, width))))
    scratch = [
        pltpu.VMEM((width, cols), bf16),
        pltpu.VMEM((LEN, cols), bf16),
        pltpu.VMEM((128, LEN), f32),
        pltpu.VMEM((128, LEN), f32),
        pltpu.SemaphoreType.DMA((len(pieces),)),
    ]
    kernel = functools.partial(attend_kernel, len(pieces))
    return call(kernel, "attend", (part // 128,), [info], ins, outs, 40, scratch)


def norm_kernel(info_ref, x_ref, vec_ref, out_ref, own_ref):
    values = x_ref[0].astype(f32)
    centred = values - jnp.mean(values, -1, keepdims=True)
    spread = jnp.mean(centred * centred, -1, keepdims=True)
    normed = centred * lax.rsqrt(spread + norm_eps) * vec_ref[0:1, :] + vec_ref[1:2, :]
    low = normed.astype(bf16)
    out_ref[0] = low

    @pl.when(lax.rem(pl.program_id(0), 2) == info_ref[0])
    def _():
        own_ref[0] = low


def norm(info, tokens, vectors, deps=()):
    seqs, local, width = tokens.shape
    each = pl.BlockSpec((1, local, width), lambda i, s: (i, 0, 0))
    half = pl.BlockSpec((1, local, width), lambda i, s: (i // 2, 0, 0))
    ins = [(tokens, each), (vectors, whole(vectors.shape))]
    outs = [((tokens.shape, bf16), each), (((seqs // 2, local, width), bf16), half)]
    return call(norm_kernel, "norm", (seqs,), [info], ins, outs, 100, deps=deps)


def norm_back_kernel(order_ref, x_ref, cot_ref, vec_ref, bias_a_ref, bias_b_ref, back_ref, *rest):
    out_ref, sums_ref = rest[-2:]
    values = x_ref[0].astype(f32)
    centred = values - jnp.mean(values, -1, keepdims=True)
    spread = jnp.mean(centred * centred, -1, keepdims=True)
    scale = lax.rsqrt(spread + norm_eps)
    xhat = centred * scale
    back = back_ref[0].astype(f32)
    scaled = back * vec_ref[0:1, :]
    shift = jnp.mean(scaled, -1, keepdims=True)
    slope = jnp.mean(scaled * xhat, -1, keepdims=True)
    cot = cot_ref[0].astype(f32)
    out_ref[0] = cot + (scaled - shift - xhat * slope) * scale

    @pl.when(pl.program_id(0) == 0)
    def _():
        sums_ref[...] = jnp.zeros_like(sums_ref)
        width, half = x_ref.shape[2], bias_a_ref.shape[1]
        sums_ref[3:4, 0:half] = bias_a_ref[...]
        row, lane = 3 + half // width, half % width
        sums_ref[row : row + 1, lane : lane + half] = bias_b_ref[...]

    sums_ref[0:1, :] += jnp.sum(back * xhat, 0, keepdims=True)
    sums_ref[1:2, :] += jnp.sum(back, 0, keepdims=True)
    sums_ref[2:3, :] += jnp.sum(cot, 0, keepdims=True)


def norm_back(order, tokens, cotangent, back_normed, vectors, bias_sums, deps=(), earlier=None):
    seqs, local, width = tokens.shape
    count = back_normed.shape[0]
    picked = pl.BlockSpec((1, local, width), lambda i, s: (s[i], 0, 0))
    here = pl.BlockSpec((1, local, width), lambda i, s: (i, 0, 0))
    ins = [(tokens, picked), (cotangent, picked), (vectors, whole(vectors.shape))]
    ins += [(one, whole(one.shape)) for one in bias_sums] + [(back_normed, here)]
    alias = {}
    if earlier is not None:
        alias = {1 + len(ins): 0}
        ins.append((earlier, anywhere))
    outs = [((tokens.shape, f32), picked), (((8, width), f32), whole((8, width)))]
    return call(norm_back_kernel, "norm_back", (count,), [order], ins, outs, 7, deps=deps, alias=alias)


def back_context_kernel(pieces, column, info_ref, cot_ref, *rest):
    piece_refs, (out_ref, w_ref, sem) = rest[:pieces], rest[pieces:]
    local = out_ref.shape[2]

    @pl.when(pl.program_id(0) == 0)
    def _():
        for copy in load_pieces(info_ref[1], piece_refs, w_ref, sem, column):
            copy.wait()

    values = mm(cot_ref[...].reshape(2 * local, -1), w_ref[...]).astype(bf16)
    ahead = info_ref[4] == 0
    out_ref[0, 0] = jnp.where(ahead, values[:local], values[local:])
    out_ref[0, 1] = jnp.where(ahead, values[local:], values[:local])


def back_context_rows(info, cotangent, weights, column):
    seqs, local, width = cotangent.shape
    part = weights[0].shape[1] - column
    ins = [(cotangent, pl.BlockSpec((2, local, width), lambda i, s: (i, 0, 0)))]
    ins += [(piece, anywhere) for piece in weights]
    outs = [(((seqs // 2, 2, local, part), bf16), pl.BlockSpec((1, 2, local, part), lambda i, s: (i, 0, 0, 0)))]
    scratch = [pltpu.VMEM((width, part), bf16), pltpu.SemaphoreType.DMA((len(weights),))]
    kernel = functools.partial(back_context_kernel, len(weights), column)
    return call(kernel, "back_context", (seqs // 2,), [info], ins, outs, 6, scratch)


def feed_kernel(pieces, earlier, info_ref, x_ref, cot_ref, bias_ref, *rest):
    before, rest = rest[:earlier], rest[earlier:]
    piece_refs, rest = rest[:pieces], rest[pieces:]
    branch_ref, own_ref, away_ref, sums_ref, mine_ref, theirs_ref = rest[:6]
    w_ref, up_grad, down_grad, stage_ref, sem, out_sem = rest[6:]
    step = pl.program_id(0)
    width, hidden = up_grad.shape
    dp_index = info_ref[1]

    @pl.when(step == 0)
    def _():
        copies = load_pieces(dp_index, piece_refs, w_ref, sem)
        up_grad[...] = jnp.zeros_like(up_grad)
        down_grad[...] = jnp.zeros_like(down_grad)
        sums_ref[...] = jnp.zeros_like(sums_ref)
        for copy in copies:
            copy.wait()

    x = x_ref[...].reshape(-1, width)
    cot = cot_ref[...].reshape(-1, width)
    x_turned, cot_turned = x.T, cot.T
    rate = math.sqrt(2.0 / math.pi)
    back = jnp.zeros(x.shape, f32)
    branch = jnp.zeros(x.shape, f32)
    chunk = min(CHUNK, hidden)
    for at in range(0, hidden, chunk):
        cols = slice(at, at + chunk)
        up, down = w_ref[:, cols], w_ref[:, hidden + at : hidden + at + chunk]
        pre = mm(x, up) + bias_ref[:, cols]
        back_active = mm(cot, down)
        square = pre * pre
        bent = jnp.tanh(rate * pre * (1.0 + 0.044715 * square))
        half = 0.5 * (1.0 + bent)
        active = (pre * half).astype(bf16)
        slope = half + 0.5 * pre * (1.0 - bent * bent) * (rate * (1.0 + 3 * 0.044715 * square))
        grad_pre = (back_active * slope).astype(bf16)
        sums_ref[:, cols] += jnp.sum(grad_pre.astype(f32), 0, keepdims=True)
        branch += mm(active, down, NT)
        back += mm(grad_pre, up, NT)
        up_grad[:, cols] += mm(x_turned, grad_pre)
        down_grad[:, cols] += mm(cot_turned, active)
    if earlier:
        branch += before[0][...]
    branch_ref[...] = branch
    local = own_ref.shape[1]
    even = info_ref[0] == 0
    own = jnp.where(even, back[:local], back[local:])
    away = jnp.where(even, back[local:], back[:local])
    if earlier:
        own += before[1][0]
        away += before[2][0]
    own_ref[0] = own.astype(own_ref.dtype)
    away_ref[0] = away.astype(away_ref.dtype)

    @pl.when(step == pl.num_programs(0) - 1)
    def _():
        blocks = owner_blocks()
        rows = width // (2 * len(blocks))
        copies = []
        for number, (dp_half, seq) in enumerate(blocks):
            to = pl.ds(number * rows, rows)
            spot = owner_rows(info_ref, dp_half, seq, 1, rows)
            stage_ref[to, :hidden] = up_grad[spot, :].astype(bf16)
            stage_ref[to, hidden:] = down_grad[spot, :].astype(bf16)
            spot = owner_rows(info_ref, dp_half, seq, 0, rows)
            for side, source in enumerate((up_grad, down_grad)):
                target = mine_ref.at[to, pl.ds(side * hidden, hidden)]
                copies.append(pltpu.make_async_copy(source.at[spot], target, out_sem.at[2 * number + side]))
        copies.append(pltpu.make_async_copy(stage_ref, theirs_ref, out_sem.at[2 * len(blocks)]))
        for copy in copies:
            copy.start()
        for copy in copies:
            copy.wait()


def feed(info, normed, cotangent, bias, weights, before=(), deps=()):
    seqs, local, width = normed.shape
    rows, hidden = weights[0].shape[0], weights[0].shape[1] // 2
    pieces = len(weights)
    pair = pl.BlockSpec((2, local, width), lambda i, s: (i, 0, 0))
    half = pl.BlockSpec((1, local, width), lambda i, s: (i, 0, 0))
    flat = pl.BlockSpec((2 * local, width), lambda i, s: (i, 0))
    term_rows = pieces // 2 * rows
    kind = bf16 if before else f32
    ins = [(normed, pair), (cotangent, pair), (bias, whole((1, hidden)))]
    ins += list(zip(before, [flat, half, half])) + [(piece, anywhere) for piece in weights]
    outs = [
        (((seqs * local, width), f32), flat),
        (((seqs // 2, local, width), kind), half),
        (((seqs // 2, local, width), kind), half),
        (((1, hidden), f32), whole((1, hidden))),
        (((term_rows, 2 * hidden), f32), anywhere),
        (((term_rows, 2 * hidden), bf16), anywhere),
    ]
    scratch = [
        pltpu.VMEM((width, 2 * hidden), bf16),
        pltpu.VMEM((width, hidden), f32),
        pltpu.VMEM((width, hidden), f32),
        pltpu.VMEM((term_rows, 2 * hidden), bf16),
        pltpu.SemaphoreType.DMA((pieces,)),
        pltpu.SemaphoreType.DMA((2 * len(owner_blocks()) + 1,)),
    ]
    kernel = functools.partial(feed_kernel, pieces, len(before))
    return call(kernel, "feed", (seqs // 2,), [info], ins, outs, 37, scratch, deps)


def split_term(info_ref, sum_ref, mine_ref, theirs_ref):
    blocks = owner_blocks()
    rows = sum_ref.shape[0] // (2 * len(blocks))
    for number, (dp_half, seq) in enumerate(blocks):
        to = slice(number * rows, (number + 1) * rows)
        mine_ref[to, :] = sum_ref[owner_rows(info_ref, dp_half, seq, 0, rows), :]
        theirs_ref[to, :] = sum_ref[owner_rows(info_ref, dp_half, seq, 1, rows), :].astype(bf16)


def branch_kernel(last, pieces, column, order_ref, info_ref, context_ref, feed_ref, cot_ref, *rest):
    piece_refs, rest = rest[:pieces], rest[pieces:]
    before_ref = rest[0]
    own_ref, away_ref, rest = rest[last], rest[last + 1], rest[last + 2 :]
    w_ref, sem = rest[-2:]
    sum_ref = rest[-3]
    step = pl.program_id(0)

    @pl.when(step == 0)
    def _():
        for copy in load_pieces(info_ref[1], piece_refs, w_ref, sem, column):
            copy.wait()

    context = context_ref[0]
    share = own_ref.shape[2]
    own = pl.ds(pl.multiple_of(info_ref[2] * share, share), share)
    away = pl.ds(pl.multiple_of((1 - info_ref[2]) * share, share), share)
    own_ref[0] = feed_ref[0, :, own] + mm(context, w_ref[own, :], NT)
    away_ref[0] = (feed_ref[0, :, away] + mm(context, w_ref[away, :], NT)).astype(bf16)
    term = mm(cot_ref[0], context, TN)

    @pl.when(step == 0)
    def _():
        sum_ref[...] = term + before_ref[...] if last else term

    @pl.when(step > 0)
    def _():
        sum_ref[...] += term

    if last:

        @pl.when(step == pl.num_programs(0) - 1)
        def _():
            split_term(info_ref, sum_ref, *rest[:2])


def branch_rows(order, info, context, feed_branch, cotangent, weights, column, deps, before=None):
    count, local, part = context.shape
    width = cotangent.shape[2]
    last = before is not None
    half = pl.BlockSpec((1, local, width // 2), lambda i, s, t: (i, 0, 0))
    picked = pl.BlockSpec((1, local, width), lambda i, s, t: (s[i], 0, 0))
    ins = [(context, pl.BlockSpec((1, local, part), lambda i, s, t: (i, 0, 0)))]
    ins += [(feed_branch, picked), (cotangent, picked)] + [(piece, anywhere) for piece in weights]
    if last:
        ins.append((before, whole(before.shape)))
    terms = [((width // 2, part), f32), ((width // 2, part), bf16)] if last else [((width, part), f32)]
    outs = [(((count, local, width // 2), kind), half) for kind in (f32, bf16)]
    outs += [(term, whole(term[0])) for term in terms]
    scratch = [pltpu.VMEM((width, part), f32)] * last
    scratch += [pltpu.VMEM((width, part), bf16), pltpu.SemaphoreType.DMA((len(weights),))]
    kernel = functools.partial(branch_kernel, int(last), len(weights), column)
    return call(kernel, "branch", (count,), [order, info], ins, outs, 9, scratch, deps)


def output_kernel(info_ref, x_ref, own_ref, own_got_ref, other_ref, other_got_ref, vec_ref, out_ref):
    even = info_ref[0] == 0
    own = own_ref[0] + own_got_ref[0].astype(f32)
    other = other_ref[0] + other_got_ref[0].astype(f32)
    total = jnp.concatenate([jnp.where(even, own, other), jnp.where(even, other, own)], axis=0)
    out_ref[...] = (x_ref[...].astype(f32) + total + vec_ref[2:3, :]).astype(bf16)


def output_rows(info, tokens, own, own_got, other, other_got, params_here, deps):
    seqs, local, width = tokens.shape
    share = own.shape[2]
    half = pl.BlockSpec((1, local, share), lambda i, s: (i, 0, 0))
    ins = [(tokens.reshape(-1, width), pl.BlockSpec((2 * local, share), lambda i, s: (i, s[2])))]
    ins += [(one, half) for one in (own, own_got, other, other_got)] + [(params_here, whole(params_here.shape))]
    outs = [(((seqs * local, share), bf16), pl.BlockSpec((2 * local, share), lambda i, s: (i, 0)))]
    return call(output_kernel, "output", (seqs // 2,), [info], ins, outs, 6, deps=deps)[0]


def joint_term_kernel(count, info_ref, *refs):
    xs, grads, (mine_ref, theirs_ref, sum_ref) = refs[:count], refs[count : 2 * count], refs[2 * count :]
    term = mm(xs[0][...], grads[0][...], TN)
    for x, grad in zip(xs[1:], grads[1:]):
        term += mm(x[...], grad[...], TN)
    sum_ref[...] = term
    steps = pl.num_programs(0) // 2
    order = seq_order()
    rows = term.shape[0] // len(order)
    parts = [sum_ref[pl.ds(pl.multiple_of((info_ref[3] ^ seq) * rows, rows), rows), :] for seq in order]

    @pl.when(pl.program_id(0) < steps)
    def _():
        for number, part in enumerate(parts):
            theirs_ref[number * rows : (number + 1) * rows, :] = part.astype(bf16)

    @pl.when(pl.program_id(0) >= steps)
    def _():
        for number, part in enumerate(parts):
            mine_ref[number * rows : (number + 1) * rows, :] = part


def joint_term(info, xs, grads, deps):
    pieces = lax.axis_size("dp")
    steps = pieces // 2
    width, cols = xs[0].shape[1], grads[0].shape[1]
    rows = width // pieces

    def picked(i, s):
        return (0, s[1] ^ (2 * lax.rem(i, steps) + 1 - i // steps))

    ins = [(x, pl.BlockSpec((LEN, rows), picked)) for x in xs] + [(grad, whole((LEN, cols))) for grad in grads]
    outs = [
        (((steps * rows, cols), f32), pl.BlockSpec((rows, cols), lambda i, s: (jnp.maximum(i - steps, 0), 0))),
        (((steps * rows, cols), bf16), pl.BlockSpec((rows, cols), lambda i, s: (jnp.minimum(i, steps - 1), 0))),
    ]
    scratch = [pltpu.VMEM((rows, cols), f32)]
    kernel = functools.partial(joint_term_kernel, len(xs))
    return call(kernel, "joint_term", (pieces,), [info], ins, outs, 12, scratch, deps)


def halves(values):
    high = values.astype(bf16)
    return high, (values - high.astype(f32)).astype(bf16)


def mm3(a, b, dims):
    a_high, a_low = a
    b_high, b_low = b
    return mm(a_high, b_high, dims) + (mm(a_high, b_low, dims) + mm(a_low, b_high, dims))


def shampoo_kernel(fan, flipped, g_ref, w_ref, big_ref, small_ref, root_ref, small_root_ref, *rest):
    big_out, small_out, w_out, left_ref, right_ref, sg_ref, turned_ref = rest
    step = pl.program_id(0)
    rows, block = g_ref.shape[0], big_ref.shape[0]
    cols = pl.ds(pl.multiple_of(step * block, block), block)

    @pl.when(step == 0)
    def _():
        g = halves(g_ref[...])
        left_ref[...] = jnp.concatenate([g[0], g[1], g[0]], axis=0)
        right_ref[...] = jnp.concatenate([g[0], g[0], g[1]], axis=0)
        turned = mm3(halves(small_root_ref[...]), g, TN if flipped else NN)
        sg_ref[...] = jnp.concatenate(halves(turned), axis=0)
        small_out[...] = beta_stats * small_ref[...] + (1.0 - beta_stats) * mm3(g, g, NT)

    big_out[...] = beta_stats * big_ref[...] + (1.0 - beta_stats) * mm(left_ref[:, cols], right_ref[...], TN)
    root_high, root_low = halves(root_ref[...])
    if flipped:
        both = mm(sg_ref[...], root_high, NT)
        turned_ref[:, cols] = both[:rows] + both[rows:] + mm(sg_ref[:rows, :], root_low, NT)
    else:
        both = mm(sg_ref[:, cols], root_high)
        part = both[:rows] + both[rows:] + mm(sg_ref[:rows, cols], root_low)

        @pl.when(step == 0)
        def _():
            turned_ref[...] = part

        @pl.when(step > 0)
        def _():
            turned_ref[...] += part

    @pl.when(step == pl.num_programs(0) - 1)
    def _():
        turned = turned_ref[...]
        square = jnp.sum(turned * turned, axis=(0, 1), keepdims=True) * (1.0 / turned.size)
        w_out[...] = w_ref[...] - rate_matrix / math.sqrt(fan) * turned * lax.rsqrt(square + 1e-06)


def shampoo(gradient, weight, big, small, big_root, small_root, fan, flipped, deps=()):
    rows, size = gradient.shape
    block = min(STRIP, size)
    if size % block:
        block = size
    strip = pl.BlockSpec((block, size), lambda i: (i, 0))
    square = whole((rows, rows))
    flat = whole((rows, size))
    ins = [(gradient, flat), (weight, flat), (big, strip), (small, square), (big_root, strip), (small_root, square)]
    outs = [(((size, size), f32), strip), (((rows, rows), f32), square), (((rows, size), f32), flat)]
    scratch = [
        pltpu.VMEM((3 * rows, size), bf16),
        pltpu.VMEM((3 * rows, size), bf16),
        pltpu.VMEM((2 * rows, size), bf16),
        pltpu.VMEM((rows, size), f32),
    ]
    kernel = functools.partial(shampoo_kernel, fan, flipped)
    return call(kernel, "shampoo", (size // block,), [], ins, outs, 19 * size * size / 2048**2, scratch, deps)


def diagonal_rule(values, moment, gradient):
    moment_new = beta_moment * moment + (1.0 - beta_moment) * gradient * gradient
    return (moment_new, values - rate_vector * gradient / (jnp.sqrt(moment_new) + 1e-08))


def body(
    tokens,
    cotangent,
    lengths,
    orientation,
    joint_weight,
    output_weight,
    expand_weight,
    shrink_weight,
    norm_params,
    expand_bias,
    norm_moment,
    bias_moment,
    joint_left,
    joint_right,
    joint_left_root,
    joint_right_root,
    output_left,
    output_right,
    output_left_root,
    output_right_root,
    expand_left,
    expand_right,
    expand_left_root,
    expand_right_root,
    shrink_left,
    shrink_right,
    shrink_left_root,
    shrink_right_root,
):
    n_mp, n_seq, n_dp = lax.axis_size("mp"), lax.axis_size("seq"), lax.axis_size("dp")
    mp_index, seq_index, dp_index = lax.axis_index("mp"), lax.axis_index("seq"), lax.axis_index("dp")
    seqs, local, width = tokens.shape
    rows = seqs * local
    share = norm_params.shape[1]
    per = seqs // n_seq
    paired = n_mp == 2 and per == 2
    flip = mp_index if paired else jnp.zeros((), jnp.int32)
    ids = [1 - flip, flip] if paired else list(range(per))
    info = jnp.stack([flip, dp_index, mp_index, seq_index, jnp.asarray(ids[0])]).astype(jnp.int32)

    def facts(which):
        spot = seq_index * per + which
        values = [lax.dynamic_index_in_dim(one, spot, 0, False) for one in (lengths, orientation)]
        return jnp.stack(values + [dp_index])

    def own_share(values):
        return lax.dynamic_slice_in_dim(values, mp_index * share, share, values.ndim - 1)

    def to_whole(values):
        return lax.all_to_all(values, "seq", 0, 0, tiled=True)

    output_t, shrink_t = output_weight.T, shrink_weight.T
    hidden = expand_weight.shape[1]
    half = hidden // 2
    both = lambda left, right: jnp.concatenate([left.astype(bf16), right.astype(bf16)], axis=1)
    early = Gather(both(expand_weight[:, :half], shrink_t[:, :half]))
    middle = Gather(both(joint_weight, output_t))
    late = Gather(both(expand_weight[:, half:], shrink_t[:, half:]))
    along = len(bits_of(n_seq))

    early.value, params_here = tie(early.value, norm_params)
    if paired:
        other_params = swap(params_here, "mp", 1)
        upper = mp_index != 0
        vectors = jnp.concatenate(
            [jnp.where(upper, other_params, norm_params), jnp.where(upper, norm_params, other_params)], axis=1
        )
    else:
        vectors = lax.all_gather(params_here, "mp", axis=1, tiled=True)
    tables = rope_tables()
    facts_of = [facts(which) for which in ids]
    normed, normed_own = norm(info, tokens, vectors)
    early.step()
    early.value, middle.value, late.value, normed, normed_own = tie(
        early.value, middle.value, late.value, normed, normed_own
    )
    for _ in range(1, along):
        early.step()
    middle.step()
    early.value, middle.value, late.value = tie(early.value, middle.value, late.value)
    while len(early.todo) > 1:
        early.step()
    for _ in range(1, along):
        middle.step()
    for _ in range(along):
        late.step()
    (middle.value, late.value, normed_own), (early.pieces,) = beside(
        [middle.value, late.value, normed_own], early.pieces
    )
    early.step()
    while len(middle.todo) > 1:
        middle.step()
    while len(late.todo) > 1:
        late.step()
    (normed_own,), (early.pieces, tables, facts_of) = beside([normed_own], early.pieces, list(tables), facts_of)

    if paired:
        arrived = [to_whole(normed_own).reshape(LEN, width)]
    else:
        split = normed.reshape(n_seq, per, local, width)
        arrived = [to_whole(split[:, t]).reshape(LEN, width) for t in range(per)]

    first = feed(info, normed, cotangent, expand_bias[None, :half], early.pieces, deps=[late.pieces[0]])
    first, (middle.pieces, late.pieces) = beside(first, middle.pieces, late.pieces)
    middle.step()
    scatter_early = Scatter(first[4], first[5])
    (scatter_early.away,), (middle.pieces, late.pieces, arrived) = beside(
        [scatter_early.away], middle.pieces, late.pieces, arrived
    )
    late.step()
    scatter_early.step()
    normed_seqs = [swap(arrived[0], "mp", 1), arrived[0]] if paired else arrived
    joint_cols = joint_weight.shape[1]
    part = joint_cols // 3
    back_parts = back_context_rows(info, cotangent, middle.pieces, joint_cols)
    back_parts, (late.pieces, scatter_early.terms[-1]) = beside(back_parts, late.pieces, scatter_early.terms[-1])
    back_whole = to_whole(back_parts[0])
    scatter_early.step()
    second = feed(info, normed, cotangent, expand_bias[None, half:], late.pieces, first[:3])
    second, (normed_seqs, back_whole, scatter_early.terms[-1]) = beside(
        second, normed_seqs, back_whole, scatter_early.terms[-1]
    )
    feed_branch, ffn_own, ffn_away = second[:3]
    known = [first[3], second[3]]

    fans = (width, width // 32, width, 4 * width)
    expand_state = (expand_weight, expand_right, expand_left, expand_right_root, expand_left_root, fans[2], False)
    shrink_state = (shrink_t, shrink_left, shrink_right, shrink_left_root, shrink_right_root, fans[3], True)
    joint_state = (joint_weight, joint_right, joint_left, joint_right_root, joint_left_root, fans[0], False)
    output_state = (output_t, output_left, output_right, output_left_root, output_right_root, fans[1], True)
    kind = bf16 if paired else f32
    scatter_late = Scatter(second[4], second[5])
    scatter_late.step()
    scatter_early.step()
    scatter_late.step()
    attended = attend(facts_of[0], normed_seqs[0], middle.pieces, back_whole, 0, tables, kind)
    attended, (scatter_early.terms[-1], scatter_late.terms[-1]) = beside(
        attended, scatter_early.terms[-1], scatter_late.terms[-1]
    )
    context_other, grad_other, back_other = attended
    received = [swap(back_other, "mp", 1)] if paired else []
    context_other = to_whole(context_other.reshape(n_seq, local, part))
    scatter_early.step()
    scatter_late.step()
    attended = attend(facts_of[1], normed_seqs[1], middle.pieces, back_whole, 1, tables, kind)
    attended, (ffn_away, received, context_other, scatter_early.terms[-1], scatter_late.terms[-1]) = beside(
        attended, ffn_away, received, context_other, scatter_early.terms[-1], scatter_late.terms[-1]
    )
    context_own, grad_own, back_own = attended
    context_own = context_own.reshape(n_seq, local, part)
    grads = [grad_other, grad_own]

    def feed_grads():
        early_grad, late_grad = scatter_early.finish(), scatter_late.finish()
        expand_grad = jnp.concatenate([early_grad[:, :half], late_grad[:, :half]], axis=1)
        return expand_grad, jnp.concatenate([early_grad[:, half:], late_grad[:, half:]], axis=1)

    if paired:
        order = jnp.arange(n_seq, dtype=jnp.int32) * 2
        own_order, other_order = order + flip, order + 1 - flip
        back_sum = (back_own.astype(f32) + received[0].astype(f32)).astype(bf16)
        scatter_late.step()
        ffn_got = swap(ffn_away, "mp", 1)
        context_own = to_whole(context_own)
        branch_in = feed_branch.reshape(tokens.shape)
        branched = branch_rows(
            other_order, info, context_other, branch_in, cotangent, middle.pieces, joint_cols, [back_sum]
        )
        other_own, other_away, output_term = branched
        own_got = swap(other_away, "mp", 1)
        joint_parts = joint_term(info, normed_seqs, grads, [output_term])
        joint_parts, (context_own, back_sum) = beside(joint_parts, context_own, back_sum)
        back_sum = to_whole(back_sum.reshape(n_seq, local, width))
        expand_grad, shrink_grad = feed_grads()
        scatter_joint = Scatter(*joint_parts)
        scatter_joint.step()
        expand_new = shampoo(expand_grad, *expand_state, [joint_parts[0]])
        expand_new, (scatter_joint.terms[-1], ffn_got) = beside(expand_new, scatter_joint.terms[-1], ffn_got)
        scatter_joint.step()
        branched = branch_rows(
            own_order, info, context_own, branch_in, cotangent, middle.pieces, joint_cols, [expand_new[1]], output_term
        )
        own_own, own_away, output_mine, output_theirs = branched
        other_got = swap(own_away, "mp", 1)
        scatter_output = Scatter(output_mine, output_theirs)
        scatter_output.step()
        shrink_new = shampoo(shrink_grad, *shrink_state, [output_mine])
        shrink_new, (back_sum, scatter_joint.terms[-1], scatter_output.terms[-1]) = beside(
            shrink_new, back_sum, scatter_joint.terms[-1], scatter_output.terms[-1]
        )
        scatter_joint.step()
        scatter_output.step()
        total = ffn_own.astype(f32) + ffn_got.astype(f32) + back_sum.astype(f32)
        total = total.astype(bf16)
        total_other = swap(total, "mp", 1)
        backed = norm_back(own_order, tokens, cotangent, total, vectors, known, [shrink_new[1]])
        backed, (scatter_joint.terms[-1], scatter_output.terms[-1], own_got, other_got) = beside(
            backed, scatter_joint.terms[-1], scatter_output.terms[-1], own_got, other_got
        )
        input_grad, sums = backed
        hops = [(axis, bit) for axis in ("dp", "seq") for bit in bits_of(lax.axis_size(axis))]
        vector_terms = sums
        vector_got = swap(vector_terms, *hops[0])
        scatter_joint.step()
        vector_got, scatter_output.terms[-1] = tie(vector_got, scatter_output.terms[-1])
        vector_terms = vector_terms + vector_got
        vector_got = swap(vector_terms, *hops[1])
        scatter_output.step()
        block_output = output_rows(
            info, tokens, own_own, own_got, other_own, other_got, norm_params, [sums]
        )
        (block_output,), (scatter_joint.terms[-1], scatter_output.terms[-1], vector_got) = beside(
            [block_output], scatter_joint.terms[-1], scatter_output.terms[-1], vector_got
        )
        block_output = block_output.reshape(seqs, local, share)
        vector_terms = vector_terms + vector_got
        vector_got = swap(vector_terms, *hops[2])
        joint_grad = scatter_joint.finish()
        scatter_output.step()
        joint_new = shampoo(joint_grad, *joint_state, [block_output])
        joint_new, (scatter_output.terms[-1], vector_got) = beside(
            joint_new, scatter_output.terms[-1], vector_got
        )
        vector_terms = vector_terms + vector_got
        vector_got = swap(vector_terms, *hops[3])
        output_grad = scatter_output.finish()
        output_new = shampoo(output_grad, *output_state, [joint_new[1]])
        output_new, (total_other, vector_got) = beside(output_new, total_other, vector_got)
        vector_terms = vector_terms + vector_got
        for hop in hops[4:]:
            vector_terms = vector_terms + swap(vector_terms, *hop)
        sums, bias_grad = vector_terms[:3], vector_terms[3:].reshape(-1)[:hidden]
        away_share = lax.dynamic_slice_in_dim(sums, (1 - mp_index) * share, share, 1)
        share_got = swap(away_share, "mp", 1)
        backed = norm_back(other_order, tokens, cotangent, total_other, vectors, known, [], input_grad)
        (input_grad, _), (share_got,) = beside(backed, share_got)
        norm_grad = own_share(sums) + share_got
    else:
        context_own = to_whole(context_own)
        context = jnp.stack([context_other, context_own], axis=1).reshape(rows, part)
        output_full = merge_pieces([piece[:, joint_cols:] for piece in middle.pieces])
        branch = feed_branch + mm(context, output_full, NT)
        summed = lax.psum_scatter(branch, "mp", scatter_dimension=1, tiled=True).reshape(seqs, local, share)
        block_output = (own_share(tokens).astype(f32) + summed + norm_params[2]).astype(bf16)
        output_term = mm(cotangent.reshape(rows, width), context, TN).reshape(n_dp, n_seq, -1, part)
        pick = lambda dp_half, seq, other: output_term[dp_index ^ (2 * dp_half + other), seq_index ^ seq]
        output_mine, output_theirs = (
            jnp.concatenate([pick(*block, other) for block in owner_blocks()]) for other in (0, 1)
        )
        back = [lax.psum(one, "mp") for one in (back_other, back_own)]
        back = [to_whole(one.astype(bf16).reshape(n_seq, local, width)) for one in back]
        feed_back = jnp.stack([ffn_own, ffn_away], axis=1).astype(f32)
        total = jnp.stack(back, axis=1).astype(f32) + lax.psum(feed_back, "mp")
        total = total.astype(bf16).reshape(seqs, local, width)
        input_grad, sums = norm_back(jnp.arange(seqs, dtype=jnp.int32), tokens, cotangent, total, vectors, known)
        joint_grad = Scatter(*joint_term(info, normed_seqs, grads, [])).finish()
        output_grad = Scatter(output_mine, output_theirs.astype(bf16)).finish()
        expand_grad, shrink_grad = feed_grads()
        expand_new = shampoo(expand_grad, *expand_state)
        shrink_new = shampoo(shrink_grad, *shrink_state)
        joint_new = shampoo(joint_grad, *joint_state)
        output_new = shampoo(output_grad, *output_state)
        vector_terms = sums
        for axis in ("dp", "seq"):
            for bit in bits_of(lax.axis_size(axis)):
                vector_terms = vector_terms + swap(vector_terms, axis, bit)
        norm_grad, bias_grad = own_share(vector_terms[:3]), vector_terms[3:].reshape(-1)[:hidden]

    joint_right_new, joint_left_new, joint_new = joint_new
    output_left_new, output_right_new, output_new = output_new
    expand_right_new, expand_left_new, expand_new = expand_new
    shrink_left_new, shrink_right_new, shrink_new = shrink_new
    norm_moment_new, norm_params_new = diagonal_rule(norm_params, norm_moment, norm_grad)
    bias_moment_new, bias_new = diagonal_rule(expand_bias, bias_moment, bias_grad)
    return (
        block_output,
        input_grad,
        joint_grad,
        output_grad.T,
        expand_grad,
        shrink_grad.T,
        norm_grad,
        bias_grad,
        joint_left_new,
        joint_right_new,
        output_left_new,
        output_right_new,
        expand_left_new,
        expand_right_new,
        shrink_left_new,
        shrink_right_new,
        joint_new,
        output_new.T,
        expand_new,
        shrink_new.T,
        norm_moment_new,
        bias_moment_new,
        norm_params_new,
        bias_new,
    )


def solution(mesh):
    data = P("dp", "seq", None)
    rows = P(("dp", "seq"), "mp")
    cols = P("mp", ("dp", "seq"))
    vector = P(None, "mp")
    placed = (data, data, P("dp"), P("dp"), rows, cols, rows, cols, vector, P("mp"), vector, P("mp")) + (rows,) * 16
    out_placed = (
        (P("dp", "seq", "mp"), data, rows, cols, rows, cols, vector, P("mp"))
        + (rows,) * 8
        + (rows, cols, rows, cols, vector, P("mp"), vector, P("mp"))
    )
    return jax.shard_map(body, mesh=mesh, in_specs=placed, out_specs=out_placed, check_vma=False)
```
